512 devices in a mesh: gx: 32 (over y, z_hi, core), gy: 16 (over x, z_lo).
Axes of the slice: x: 4, y: 4, z: 16 (z_hi: 4, z_lo: 4; z = z_hi * 4 + z_lo), core: 2. Of those that a mesh axis runs over, the one named last changes fastest.
Arguments:
- surface_tags: int32 [64, 128, 128], P('gx', 'gy'), may hold values from 0 to 16
- normal_index: int32 [64, 128, 128], P('gx', 'gy'), may hold values from 0 to 25
- fluid_mask: int32 [64, 128, 128], P('gx', 'gy'), may hold values 0 or 1
- body_centers: float32 [16, 3], replicated, may hold values from 0.25 to 0.75
Outputs:
- pressure: float32 [96, 64, 128, 128], P(None, 'gx', 'gy')
- added_mass: float32 [96, 96], replicated
The draws below stay inside these ranges and needn't reach their ends.
Inputs may be any that keep to these rules, and one draw needn't show every extreme that they name: `surface_tags`: 16 marks a cell on no body's surface.
All inputs are finite; a program needn't handle non-finite values. No bound on the sum of `fluid_mask` on one device may be relied on, other than what follows from the above.
Results may differ from the reference program's by a relative error of at most 0.00005.
Values sent between devices are 32-bit elements; how exact they have to be, the bound alone decides.
No kernel may reach another device: no remote copies, remote signals or barrier semaphores. Data moves between devices by JAX's collectives and lax.ppermute only.
A program may use at most 64 MiB of HBM per device.

```python
import jax
import jax.numpy as jnp
from jax import lax

BODIES = 16
NZ = 128
NX = 64
NY = 128


def touch_ends(values, stream_key, low, top_value):
    place = [jax.random.randint(jax.random.fold_in(stream_key, axis), (), 0, length) for axis, length in enumerate(values.shape)]
    longest = values.shape.index(max(values.shape))
    next_to = place[:longest] + [(place[longest] + 1) % values.shape[longest]] + place[longest + 1:]
    return values.at[tuple(place)].set(low).at[tuple(next_to)].set(top_value)


def setup_inputs(seed: int = 0) -> dict:
    arg_keys = jax.random.split(jax.random.key(seed), 5)
    surface_tags = touch_ends(jax.random.randint(arg_keys[0], (NX, NY, NZ), 0, BODIES + 1), jax.random.fold_in(arg_keys[0], 1), 0, BODIES).astype(jnp.int32)
    normal_index = touch_ends(jax.random.randint(arg_keys[1], (NX, NY, NZ), 0, 26), jax.random.fold_in(arg_keys[1], 1), 0, 25).astype(jnp.int32)
    fluid_mask = touch_ends((jax.random.randint(arg_keys[2], (NX, NY, NZ), 0, 8) < 7).astype(jnp.int32), jax.random.fold_in(arg_keys[2], 1), 0, 1)
    body_centers = jnp.clip(jax.random.uniform(arg_keys[3], (BODIES, 3), jnp.float32, 0.25, 0.75), 0.25, 0.75)
    return dict(surface_tags=surface_tags, normal_index=normal_index, fluid_mask=fluid_mask, body_centers=body_centers)


def normals_of(index):
    shifted = index + (index >= 13).astype(jnp.int32)
    comp_x = (shifted // 9 - 1).astype(jnp.float32)
    comp_y = (shifted // 3 % 3 - 1).astype(jnp.float32)
    comp_z = (shifted % 3 - 1).astype(jnp.float32)
    length = jnp.sqrt(comp_x * comp_x + comp_y * comp_y + comp_z * comp_z)
    return (comp_x / length, comp_y / length, comp_z / length)

def forcing_of(tags, index, fluid, centers, pos_x, pos_y, pos_z):
    n_x, n_y, n_z = normals_of(index)
    shape = (BODIES,) + tags.shape
    bodies = jnp.arange(BODIES, dtype=jnp.int32)
    onehot = (tags[None] == bodies[:, None, None, None]).astype(jnp.float32) * fluid[None]
    lever_x = 3.0 * (pos_x[None, :, None, None] - centers[:, 0][:, None, None, None])
    lever_y = 3.0 * (pos_y[None, None, :, None] - centers[:, 1][:, None, None, None])
    lever_z = 3.0 * (pos_z[None, None, None, :] - centers[:, 2][:, None, None, None])
    parts = [n_x[None], n_y[None], n_z[None], lever_y * n_z[None] - lever_z * n_y[None], lever_z * n_x[None] - lever_x * n_z[None], lever_x * n_y[None] - lever_y * n_x[None]]
    modes = jnp.stack([jnp.broadcast_to(part, shape) for part in parts], axis=1)
    modes = modes * onehot[:, None]
    return modes.reshape((6 * BODIES,) + tags.shape)

def operate(field, fluid):
    masked = fluid[None] * field
    padded = jnp.pad(masked, ((0, 0), (1, 1), (1, 1), (1, 1)))
    beside = padded[:, 2:, 1:-1, 1:-1] + padded[:, :-2, 1:-1, 1:-1]
    beside = beside + padded[:, 1:-1, 2:, 1:-1] + padded[:, 1:-1, :-2, 1:-1]
    beside = beside + padded[:, 1:-1, 1:-1, 2:] + padded[:, 1:-1, 1:-1, :-2]
    return fluid[None] * (6.0 * field - beside) + (1.0 - fluid[None]) * field

def gram(left, right):
    return jnp.einsum('rxyz,sxyz->rs', left, right, precision=lax.Precision.HIGHEST)

def combine(field, coeffs):
    return jnp.einsum('rxyz,rs->sxyz', field, coeffs, precision=lax.Precision.HIGHEST)

def solve_spd(matrix, rhs_mat):
    sym = 0.5 * (matrix + matrix.T)
    factor = jnp.linalg.cholesky(sym)
    inner = lax.linalg.triangular_solve(factor, rhs_mat, left_side=True, lower=True)
    return lax.linalg.triangular_solve(factor, inner, left_side=True, lower=True, transpose_a=True)

def reference(surface_tags, normal_index, fluid_mask, body_centers):
    fluid = fluid_mask.astype(jnp.float32)
    pos_x = (jnp.arange(NX).astype(jnp.float32) + 0.5) / NX
    pos_y = (jnp.arange(NY).astype(jnp.float32) + 0.5) / NY
    pos_z = (jnp.arange(NZ).astype(jnp.float32) + 0.5) / NZ
    forcing = forcing_of(surface_tags, normal_index, fluid, body_centers, pos_x, pos_y, pos_z)
    rr0 = gram(forcing, forcing)
    q0 = operate(forcing, fluid)
    alpha0 = solve_spd(gram(forcing, q0), rr0)
    x1 = combine(forcing, alpha0)
    r1 = forcing - combine(q0, alpha0)
    q0 = None
    rr1 = gram(r1, r1)
    beta = solve_spd(rr0, rr1)
    p1 = r1 + combine(forcing, beta)
    r1 = None
    q1 = operate(p1, fluid)
    alpha1 = solve_spd(gram(p1, q1), rr1)
    q1 = None
    pressure = x1 + combine(p1, alpha1)
    added_mass = gram(forcing, pressure) * (8.0 * BODIES / (NX * NY * NZ))
    return (pressure, added_mass)
```

```python
import functools

import jax
import jax.numpy as jnp
import numpy as np
from jax import lax
from jax.experimental import pallas as pl
from jax.experimental.pallas import tpu as pltpu
from jax.sharding import Mesh, PartitionSpec as P

BODIES = 16
MODES = 6
COLS = BODIES * MODES
FOLD = 4 * MODES
GX = ("y", "zh", "c")
GY = ("x", "zl")
NEAR = ("y", "c", "x")
FAR = ("zh", "zl")
F32 = jnp.float32


def dot(left, right, dims):
    return lax.dot_general(
        left, right, (dims, ((), ())), precision=lax.Precision.HIGHEST, preferred_element_type=F32
    )


def mm(left, right):
    return dot(left, right, ((1,), (0,)))


def fields_kernel(nx, ny, nz, offs, ints, cen, lh, pay, rh, base, fext, qext, cx, cy):
    ex, ey = nx + 4, ny + 4
    tags, index, fluid = ints[0], ints[1], ints[2]
    shifted = index + (index >= 13).astype(jnp.int32)
    part_x = (shifted >= 9).astype(jnp.int32) + (shifted >= 18).astype(jnp.int32)
    rest = shifted - 9 * part_x
    part_y = (rest >= 3).astype(jnp.int32) + (rest >= 6).astype(jnp.int32)
    part_z = rest - 3 * part_y
    comps = [(part - 1).astype(F32) for part in (part_x, part_y, part_z)]
    square = comps[0] * comps[0] + comps[1] * comps[1] + comps[2] * comps[2]
    inverse = 1.0 / jnp.sqrt(square)
    fl = fluid.astype(F32)
    for m in range(3):
        base[m] = comps[m] * inverse * fl
    base[3] = fl
    base[4] = tags.astype(F32)

    col = lax.broadcasted_iota(jnp.int32, (COLS, nz), 0)
    body = (col * 43) >> 8
    mode = col - MODES * body
    bodyf = body.astype(F32)
    lane = lax.broadcasted_iota(jnp.int32, (COLS, nz), 1)
    one = [(mode == m).astype(F32) for m in range(MODES)]
    cen_x = jnp.broadcast_to(cen[:, 0:1], (COLS, nz))
    cen_y = jnp.broadcast_to(cen[:, 1:2], (COLS, nz))
    cen_z = jnp.broadcast_to(cen[:, 2:3], (COLS, nz))
    pos_z = (lane.astype(F32) + 0.5) * (1.0 / nz)
    lever_z = 3.0 * (pos_z - cen_z)
    start_x, start_y, count_x, count_y = offs[0], offs[1], offs[2], offs[3]
    coef_x0 = one[0] + one[4] * lever_z
    coef_y0 = one[1] - one[3] * lever_z
    for i in range(ex):
        pos = ((start_x + (i - 2)).astype(F32) + 0.5) / count_x.astype(F32)
        lever = 3.0 * (pos - cen_x)
        cx[0, i] = coef_y0 + one[5] * lever
        cx[1, i] = -one[4] * lever
    for j in range(ey):
        pos = ((start_y + (j - 2)).astype(F32) + 0.5) / count_y.astype(F32)
        lever = 3.0 * (pos - cen_y)
        cy[0, j] = coef_x0 - one[5] * lever
        cy[1, j] = one[2] + one[3] * lever

    def row(which, i, j):
        return jnp.broadcast_to(base[which, i, pl.ds(j, 1), :], (COLS, nz))

    def forcing_row(i, j):
        value = row(0, i, j) * cy[0, j] + row(1, i, j) * cx[0, i] + row(2, i, j) * (cy[1, j] + cx[1, i])
        fext[i, j] = jnp.where(row(4, i, j) == bodyf, value, 0.0)

    def operate(src, i, j):
        field = src[i, j]
        up = jnp.where(lane >= 1, pltpu.roll(field, 1, 1), 0.0)
        down = jnp.where(lane < nz - 1, pltpu.roll(field, nz - 1, 1), 0.0)
        beside = src[i + 1, j] + src[i - 1, j]
        beside = beside + src[i, j + 1] + src[i, j - 1]
        beside = beside + up + down
        return field + row(3, i, j) * (5.0 * field - beside)

    for i in range(ex):
        reach = 2 - max(2 - i, i - (nx + 1), 0)

        @pl.loop(2 - reach, ny + 2 + reach)
        def _(j, i=i):
            forcing_row(i, j)

    for i in range(1, ex - 1):
        reach = 1 - max(2 - i, i - (nx + 1), 0)

        @pl.loop(2 - reach, ny + 2 + reach)
        def _(j, i=i):
            qext[i, j] = operate(fext, i, j)

    for i in range(nx):

        @pl.loop(0, ny)
        def _(j, i=i):
            cells = pl.ds(pl.multiple_of((i * ny + j) * nz, nz), nz)
            forcing, field = fext[i + 2, j + 2], qext[i + 2, j + 2]
            lh[0:COLS, cells] = forcing
            lh[COLS : 2 * COLS, cells] = field
            rh[0:COLS, cells] = field
            rh[COLS : 2 * COLS, cells] = operate(qext, i + 2, j + 2)
            fold = forcing[0:FOLD]
            for k in range(1, COLS // FOLD):
                fold = fold + forcing[k * FOLD : (k + 1) * FOLD]
            rh[2 * COLS : 2 * COLS + FOLD, cells] = fold

    grams = dot(lh[...], rh[...], ((1,), (1,)))
    first, second = grams[0:COLS, 0:COLS], grams[COLS : 2 * COLS, 0:COLS]
    third = grams[COLS : 2 * COLS, COLS : 2 * COLS]
    zeroth = grams[0:COLS, 2 * COLS : 2 * COLS + FOLD]
    r = lax.broadcasted_iota(jnp.int32, (COLS, COLS), 0)
    c = lax.broadcasted_iota(jnp.int32, (COLS, COLS), 1)
    diagonal = jnp.sum(jnp.where(r == c, second, 0.0), axis=1, keepdims=True)
    pay[...] = jnp.zeros_like(pay)
    pay[0:COLS, 0:COLS] = jnp.where(r <= c, first, second)
    pay[0:COLS, COLS : COLS + FOLD] = zeroth
    pay[0:COLS, COLS + FOLD : COLS + FOLD + 1] = diagonal
    pay[COLS : 2 * COLS, 0:COLS] = third


def inverse_spd(matrix):
    size = matrix.shape[0]
    r8 = lax.broadcasted_iota(jnp.int32, (8, size), 0)
    lane = lax.broadcasted_iota(jnp.int32, (8, size), 1)
    blocks = [matrix[8 * b : 8 * b + 8] for b in range(size // 8)]
    for k in range(size):
        at, sub = k // 8, k % 8
        here = lane == k
        pivot_row = jnp.broadcast_to(blocks[at][sub : sub + 1, :], (8, size))
        pivot = jnp.broadcast_to(blocks[at][sub : sub + 1, k : k + 1], (8, size))
        recip = 1.0 / pivot
        scaled = jnp.where(here, recip, pivot_row * recip)
        new = []
        for b, block in enumerate(blocks):
            column = jnp.broadcast_to(block[:, k : k + 1], (8, size))
            kept = jnp.where(here, 0.0, block)
            if b == at:
                new.append(jnp.where(r8 == sub, scaled, kept - column * scaled))
            else:
                new.append(kept - column * scaled)
        blocks = new
    return jnp.concatenate(blocks, axis=0)


def solve_kernel(rows, nz, scale, pay, lh, out, added):
    r = lax.broadcasted_iota(jnp.int32, (COLS, COLS), 0)
    c = lax.broadcasted_iota(jnp.int32, (COLS, COLS), 1)
    both = pay[0:COLS, 0:COLS]
    both_t = both.T
    third = pay[COLS : 2 * COLS, 0:COLS]
    third = jnp.where(r <= c, third, third.T)
    first = jnp.where(r <= c, both, both_t)
    second = jnp.where(r > c, both, both_t)
    second = jnp.where(r == c, pay[0:COLS, COLS + FOLD : COLS + FOLD + 1], second)
    zeroth = pay[0:COLS, COLS : COLS + FOLD]
    zeroth = jnp.concatenate([zeroth] * (COLS // FOLD), axis=1)
    zeroth = jnp.where(((r * 43) >> 8) == ((c * 43) >> 8), zeroth, 0.0)
    first_inv = inverse_spd(first)
    left = mm(first_inv, second)
    right = mm(first_inv, zeroth)
    schur = third - mm(second, left)
    schur = 0.5 * (schur + schur.T)
    later = mm(inverse_spd(schur), first - mm(second, right))
    early = right - mm(left, later)
    added[...] = (mm(zeroth, early) + mm(first, later)) * scale
    coeffs = jnp.concatenate([early, later], axis=0)
    values = dot(coeffs, lh[...], ((0,), (0,)))
    for k in range(rows):
        out[pl.ds(k, COLS, stride=rows), :] = values[:, k * nz : (k + 1) * nz]


def halo(array, axis, dim, width):
    size, length = lax.axis_size(axis), array.shape[dim]
    up = [(i, i + 1) for i in range(size - 1)]
    down = [(j, i) for i, j in up]
    before = lax.ppermute(lax.slice_in_dim(array, length - width, length, axis=dim), axis, up)
    after = lax.ppermute(lax.slice_in_dim(array, 0, width, axis=dim), axis, down)
    return jnp.concatenate([before, array, after], axis=dim)


def reduced(part):
    near, far = (lax.axis_size(axes) for axes in (NEAR, FAR))
    rows, lanes = part.shape
    piece = lax.all_to_all(part, NEAR, 0, 0, tiled=True).reshape(near, rows // near, lanes).sum(0)
    piece = lax.all_to_all(jnp.broadcast_to(piece[None], (far,) + piece.shape), FAR, 0, 0, tiled=True).sum(0)
    return lax.all_to_all(
        jnp.broadcast_to(piece[None], (near,) + piece.shape), NEAR, 0, 0, tiled=True
    ).reshape(rows, lanes)


def shards(surface_tags, normal_index, fluid_mask, body_centers):
    nx, ny, nz = surface_tags.shape
    count_x = nx * lax.axis_size(GX)
    count_y = ny * lax.axis_size(GY)
    ints = jnp.stack([surface_tags, normal_index, fluid_mask])
    ints = halo(ints, GY, 2, 2)
    ints = halo(ints, GX, 1, 2)
    offs = jnp.stack(
        [
            lax.axis_index(GX) * nx,
            lax.axis_index(GY) * ny,
            jnp.int32(count_x),
            jnp.int32(count_y),
        ]
    ).astype(jnp.int32)
    cen = jnp.repeat(body_centers, MODES, axis=0)
    cells = nx * ny * nz
    vmem = pl.BlockSpec(memory_space=pltpu.VMEM)
    lh, pay = pl.pallas_call(
        functools.partial(fields_kernel, nx, ny, nz),
        out_shape=(
            jax.ShapeDtypeStruct((2 * COLS, cells), F32),
            jax.ShapeDtypeStruct((2 * COLS, 128), F32),
        ),
        in_specs=[pl.BlockSpec(memory_space=pltpu.SMEM), vmem, vmem],
        out_specs=(vmem, vmem),
        scratch_shapes=[
            pltpu.VMEM((2 * COLS + FOLD, cells), F32),
            pltpu.VMEM((5, nx + 4, ny + 4, nz), F32),
            pltpu.VMEM((nx + 4, ny + 4, COLS, nz), F32),
            pltpu.VMEM((nx + 4, ny + 4, COLS, nz), F32),
            pltpu.VMEM((2, nx + 4, COLS, nz), F32),
            pltpu.VMEM((2, ny + 4, COLS, nz), F32),
        ],
        compiler_params=pltpu.CompilerParams(vmem_limit_bytes=40 * 1024 * 1024),
        name="fields",
    )(offs, ints, cen)
    pay = reduced(pay)
    scale = 8.0 * BODIES / (count_x * count_y * nz)
    pressure, added = pl.pallas_call(
        functools.partial(solve_kernel, nx * ny, nz, scale),
        out_shape=(
            jax.ShapeDtypeStruct((COLS * nx * ny, nz), F32),
            jax.ShapeDtypeStruct((COLS, COLS), F32),
        ),
        in_specs=[vmem, vmem],
        out_specs=(vmem, vmem),
        compiler_params=pltpu.CompilerParams(vmem_limit_bytes=40 * 1024 * 1024),
        name="solve",
    )(pay, lh)
    return pressure.reshape(COLS, nx, ny, nz), added


def solution(mesh):
    split = Mesh(np.asarray(mesh.devices).reshape(4, 4, 2, 4, 4), GX + GY)
    return jax.shard_map(
        shards,
        mesh=split,
        in_specs=(P(GX, GY, None), P(GX, GY, None), P(GX, GY, None), P()),
        out_specs=(P(None, GX, GY, None), P()),
        check_vma=False,
    )
```

```python
import functools

import jax
import jax.numpy as jnp
import numpy as np
from jax import lax
from jax.experimental import pallas as pl
from jax.experimental.pallas import tpu as pltpu
from jax.sharding import Mesh, PartitionSpec as P

BODIES = 16
MODES = 6
COLS = BODIES * MODES
FOLD = 4 * MODES
GX = ("y", "zh", "c")
GY = ("x", "zl")
NEAR = ("y", "c", "x")
FAR = ("zh", "zl")
F32 = jnp.float32


def dot(left, right, dims):
    return lax.dot_general(
        left, right, (dims, ((), ())), precision=lax.Precision.HIGHEST, preferred_element_type=F32
    )


def mm(left, right):
    return dot(left, right, ((1,), (0,)))


def fields_kernel(nx, ny, nz, offs, ints, cen, lh, pay, rh, base, fext, qext, cx, cy):
    ex, ey = nx + 4, ny + 4
    tags, index, fluid = ints[0], ints[1], ints[2]
    shifted = index + (index >= 13).astype(jnp.int32)
    part_x = (shifted >= 9).astype(jnp.int32) + (shifted >= 18).astype(jnp.int32)
    rest = shifted - 9 * part_x
    part_y = (rest >= 3).astype(jnp.int32) + (rest >= 6).astype(jnp.int32)
    part_z = rest - 3 * part_y
    comps = [(part - 1).astype(F32) for part in (part_x, part_y, part_z)]
    square = comps[0] * comps[0] + comps[1] * comps[1] + comps[2] * comps[2]
    inverse = 1.0 / jnp.sqrt(square)
    fl = fluid.astype(F32)
    for m in range(3):
        base[m] = comps[m] * inverse * fl
    base[3] = fl
    base[4] = tags.astype(F32)

    col = lax.broadcasted_iota(jnp.int32, (COLS, nz), 0)
    body = (col * 43) >> 8
    mode = col - MODES * body
    bodyf = body.astype(F32)
    lane = lax.broadcasted_iota(jnp.int32, (COLS, nz), 1)
    one = [(mode == m).astype(F32) for m in range(MODES)]
    cen_x = jnp.broadcast_to(cen[:, 0:1], (COLS, nz))
    cen_y = jnp.broadcast_to(cen[:, 1:2], (COLS, nz))
    cen_z = jnp.broadcast_to(cen[:, 2:3], (COLS, nz))
    pos_z = (lane.astype(F32) + 0.5) * (1.0 / nz)
    lever_z = 3.0 * (pos_z - cen_z)
    start_x, start_y, count_x, count_y = offs[0], offs[1], offs[2], offs[3]
    coef_x0 = one[0] + one[4] * lever_z
    coef_y0 = one[1] - one[3] * lever_z
    for i in range(ex):
        pos = ((start_x + (i - 2)).astype(F32) + 0.5) / count_x.astype(F32)
        lever = 3.0 * (pos - cen_x)
        cx[0, i] = coef_y0 + one[5] * lever
        cx[1, i] = -one[4] * lever
    for j in range(ey):
        pos = ((start_y + (j - 2)).astype(F32) + 0.5) / count_y.astype(F32)
        lever = 3.0 * (pos - cen_y)
        cy[0, j] = coef_x0 - one[5] * lever
        cy[1, j] = one[2] + one[3] * lever

    def row(which, i, j):
        return jnp.broadcast_to(base[which, i, pl.ds(j, 1), :], (COLS, nz))

    def forcing_row(i, j):
        value = row(0, i, j) * cy[0, j] + row(1, i, j) * cx[0, i] + row(2, i, j) * (cy[1, j] + cx[1, i])
        fext[i, j] = jnp.where(row(4, i, j) == bodyf, value, 0.0)

    def operate(src, i, j):
        field = src[i, j]
        up = jnp.where(lane >= 1, pltpu.roll(field, 1, 1), 0.0)
        down = jnp.where(lane < nz - 1, pltpu.roll(field, nz - 1, 1), 0.0)
        beside = src[i + 1, j] + src[i - 1, j]
        beside = beside + src[i, j + 1] + src[i, j - 1]
        beside = beside + up + down
        return field + row(3, i, j) * (5.0 * field - beside)

    for i in range(ex):
        reach = 2 - max(2 - i, i - (nx + 1), 0)

        @pl.loop(2 - reach, ny + 2 + reach)
        def _(j, i=i):
            forcing_row(i, j)

    for i in range(1, ex - 1):
        reach = 1 - max(2 - i, i - (nx + 1), 0)

        @pl.loop(2 - reach, ny + 2 + reach)
        def _(j, i=i):
            qext[i, j] = operate(fext, i, j)

    for i in range(nx):

        @pl.loop(0, ny)
        def _(j, i=i):
            cells = pl.ds(pl.multiple_of((i * ny + j) * nz, nz), nz)
            forcing, field = fext[i + 2, j + 2], qext[i + 2, j + 2]
            lh[0:COLS, cells] = forcing
            lh[COLS : 2 * COLS, cells] = field
            rh[0:COLS, cells] = field
            rh[COLS : 2 * COLS, cells] = operate(qext, i + 2, j + 2)
            fold = forcing[0:FOLD]
            for k in range(1, COLS // FOLD):
                fold = fold + forcing[k * FOLD : (k + 1) * FOLD]
            rh[2 * COLS : 2 * COLS + FOLD, cells] = fold

    grams = dot(lh[...], rh[...], ((1,), (1,)))
    first, second = grams[0:COLS, 0:COLS], grams[COLS : 2 * COLS, 0:COLS]
    third = grams[COLS : 2 * COLS, COLS : 2 * COLS]
    zeroth = grams[0:COLS, 2 * COLS : 2 * COLS + FOLD]
    r = lax.broadcasted_iota(jnp.int32, (COLS, COLS), 0)
    c = lax.broadcasted_iota(jnp.int32, (COLS, COLS), 1)
    diagonal = jnp.sum(jnp.where(r == c, second, 0.0), axis=1, keepdims=True)
    pay[...] = jnp.zeros_like(pay)
    pay[0:COLS, 0:COLS] = jnp.where(r <= c, first, second)
    pay[0:COLS, COLS : COLS + FOLD] = zeroth
    pay[0:COLS, COLS + FOLD : COLS + FOLD + 1] = diagonal
    pay[COLS : 2 * COLS, 0:COLS] = third


def inverse_spd(matrix, work):
    size = matrix.shape[0]
    r = lax.broadcasted_iota(jnp.int32, (size, size), 0)
    c = lax.broadcasted_iota(jnp.int32, (size, size), 1)
    diagonal = jnp.where(r == c, matrix, 0.0)
    scale_r = lax.rsqrt(jnp.sum(diagonal, axis=1, keepdims=True))
    scale_c = lax.rsqrt(jnp.sum(diagonal, axis=0, keepdims=True))
    scaled = matrix * scale_r * scale_c
    bound = jnp.max(jnp.sum(jnp.abs(scaled), axis=0, keepdims=True), axis=1, keepdims=True)
    weight = jnp.minimum(1.0, 1.9 / bound)
    eye = (r == c).astype(F32)
    rest = eye - weight * scaled
    work[0:size] = eye + rest
    work[size : 2 * size] = rest

    def longer(carry):
        power = work[size : 2 * size]
        spread = jnp.sum(power * power)
        total = work[0:size]
        power = mm(power, power)
        total = total + mm(total, power)
        power = mm(power, power)
        work[0:size] = total + mm(total, power)
        work[size : 2 * size] = power
        return carry[0] + 1, spread > 1e-4

    lax.while_loop(lambda carry: (carry[0] < 14) & carry[1], longer, (jnp.int32(0), jnp.bool_(True)))
    return work[0:size] * (weight * scale_r) * scale_c


def solve_kernel(rows, nz, scale, pay, lh, out, added, work):
    r = lax.broadcasted_iota(jnp.int32, (COLS, COLS), 0)
    c = lax.broadcasted_iota(jnp.int32, (COLS, COLS), 1)
    both = pay[0:COLS, 0:COLS]
    both_t = both.T
    third = pay[COLS : 2 * COLS, 0:COLS]
    third = jnp.where(r <= c, third, third.T)
    first = jnp.where(r <= c, both, both_t)
    second = jnp.where(r > c, both, both_t)
    second = jnp.where(r == c, pay[0:COLS, COLS + FOLD : COLS + FOLD + 1], second)
    zeroth = pay[0:COLS, COLS : COLS + FOLD]
    zeroth = jnp.concatenate([zeroth] * (COLS // FOLD), axis=1)
    zeroth = jnp.where(((r * 43) >> 8) == ((c * 43) >> 8), zeroth, 0.0)
    first_inv = inverse_spd(first, work)
    left = mm(first_inv, second)
    right = mm(first_inv, zeroth)
    schur = third - mm(second, left)
    schur = 0.5 * (schur + schur.T)
    later = mm(inverse_spd(schur, work), first - mm(second, right))
    early = right - mm(left, later)
    coeffs = jnp.concatenate([early, later], axis=0)
    values = dot(coeffs, lh[...], ((0,), (0,)))
    added[...] = (mm(zeroth, early) + mm(first, later)) * scale
    for k in range(rows):
        out[pl.ds(k, COLS, stride=rows), :] = values[:, k * nz : (k + 1) * nz]


def halo(array, axis, dim, width):
    size, length = lax.axis_size(axis), array.shape[dim]
    up = [(i, i + 1) for i in range(size - 1)]
    down = [(j, i) for i, j in up]
    before = lax.ppermute(lax.slice_in_dim(array, length - width, length, axis=dim), axis, up)
    after = lax.ppermute(lax.slice_in_dim(array, 0, width, axis=dim), axis, down)
    return jnp.concatenate([before, array, after], axis=dim)


def reduced(part):
    near, far = (lax.axis_size(axes) for axes in (NEAR, FAR))
    rows, lanes = part.shape
    piece = lax.all_to_all(part, NEAR, 0, 0, tiled=True).reshape(near, rows // near, lanes).sum(0)
    piece = lax.all_to_all(jnp.broadcast_to(piece[None], (far,) + piece.shape), FAR, 0, 0, tiled=True).sum(0)
    return lax.all_to_all(
        jnp.broadcast_to(piece[None], (near,) + piece.shape), NEAR, 0, 0, tiled=True
    ).reshape(rows, lanes)


def shards(surface_tags, normal_index, fluid_mask, body_centers):
    nx, ny, nz = surface_tags.shape
    count_x = nx * lax.axis_size(GX)
    count_y = ny * lax.axis_size(GY)
    ints = jnp.stack([surface_tags, normal_index, fluid_mask])
    ints = halo(ints, GY, 2, 2)
    ints = halo(ints, GX, 1, 2)
    offs = jnp.stack(
        [
            lax.axis_index(GX) * nx,
            lax.axis_index(GY) * ny,
            jnp.int32(count_x),
            jnp.int32(count_y),
        ]
    ).astype(jnp.int32)
    cen = jnp.repeat(body_centers, MODES, axis=0)
    cells = nx * ny * nz
    vmem = pl.BlockSpec(memory_space=pltpu.VMEM)
    lh, pay = pl.pallas_call(
        functools.partial(fields_kernel, nx, ny, nz),
        out_shape=(
            jax.ShapeDtypeStruct((2 * COLS, cells), F32),
            jax.ShapeDtypeStruct((2 * COLS, 128), F32),
        ),
        in_specs=[pl.BlockSpec(memory_space=pltpu.SMEM), vmem, vmem],
        out_specs=(vmem, vmem),
        scratch_shapes=[
            pltpu.VMEM((2 * COLS + FOLD, cells), F32),
            pltpu.VMEM((5, nx + 4, ny + 4, nz), F32),
            pltpu.VMEM((nx + 4, ny + 4, COLS, nz), F32),
            pltpu.VMEM((nx + 4, ny + 4, COLS, nz), F32),
            pltpu.VMEM((2, nx + 4, COLS, nz), F32),
            pltpu.VMEM((2, ny + 4, COLS, nz), F32),
        ],
        compiler_params=pltpu.CompilerParams(vmem_limit_bytes=40 * 1024 * 1024),
        name="fields",
    )(offs, ints, cen)
    pay = reduced(pay)
    scale = 8.0 * BODIES / (count_x * count_y * nz)
    pressure, added = pl.pallas_call(
        functools.partial(solve_kernel, nx * ny, nz, scale),
        out_shape=(
            jax.ShapeDtypeStruct((COLS * nx * ny, nz), F32),
            jax.ShapeDtypeStruct((COLS, COLS), F32),
        ),
        in_specs=[vmem, vmem],
        out_specs=(vmem, vmem),
        scratch_shapes=[pltpu.VMEM((2 * COLS, COLS), F32)],
        compiler_params=pltpu.CompilerParams(vmem_limit_bytes=40 * 1024 * 1024),
        name="solve",
    )(pay, lh)
    return pressure.reshape(COLS, nx, ny, nz), added


def solution(mesh):
    split = Mesh(np.asarray(mesh.devices).reshape(4, 4, 2, 4, 4), GX + GY)
    return jax.shard_map(
        shards,
        mesh=split,
        in_specs=(P(GX, GY, None), P(GX, GY, None), P(GX, GY, None), P()),
        out_specs=(P(None, GX, GY, None), P()),
        check_vma=False,
    )
```

```python
import functools

import jax
import jax.numpy as jnp
import numpy as np
from jax import lax
from jax.experimental import pallas as pl
from jax.experimental.pallas import tpu as pltpu
from jax.sharding import Mesh, PartitionSpec as P

BODIES = 16
MODES = 6
COLS = BODIES * MODES
FOLD = 4 * MODES
GX = ("y", "zh", "c")
GY = ("x", "zl")
NEAR = ("y", "c", "x")
FAR = ("zh", "zl")
F32 = jnp.float32


def dot(left, right, dims):
    return lax.dot_general(
        left, right, (dims, ((), ())), precision=lax.Precision.HIGHEST, preferred_element_type=F32
    )


def mm(left, right):
    return dot(left, right, ((1,), (0,)))


def fields_kernel(nx, ny, nz, info, own, pair, across, even, odd, cen, lh, pay, rh, base, fext, qext, cx, cy):
    ex, ey = nx + 4, ny + 4
    start_x, start_y, count_x, count_y, core, parity = (info[k] for k in range(6))
    first_core = core == 0
    above_is_even = parity == 0
    dense_lane = lax.broadcasted_iota(jnp.int32, (1, nz), 1)

    def describe(cells, layers, rows, shifts):
        tags, index, fluid = cells
        shifted = index + (index >= 13).astype(jnp.int32)
        part_x = (shifted >= 9).astype(jnp.int32) + (shifted >= 18).astype(jnp.int32)
        rest = shifted - 9 * part_x
        part_y = (rest >= 3).astype(jnp.int32) + (rest >= 6).astype(jnp.int32)
        part_z = rest - 3 * part_y
        comps = [(part - 1).astype(F32) for part in (part_x, part_y, part_z)]
        inverse = 1.0 / jnp.sqrt(comps[0] * comps[0] + comps[1] * comps[1] + comps[2] * comps[2])
        fl = fluid.astype(F32)
        values = [comp * inverse * fl for comp in comps] + [tags.astype(F32)]
        for m, value in enumerate(values):
            base[m, layers, rows] = value
            if shifts:
                after = pltpu.roll(value, nz - 1, value.ndim - 1)
                before = pltpu.roll(value, 1, value.ndim - 1)
                if m == 3:
                    after = jnp.where(dense_lane == nz - 1, -1.0, after)
                    before = jnp.where(dense_lane == 0, -1.0, before)
                base[4 + m, layers, rows] = after
                base[8 + m, layers, rows] = before
        base[12, layers, rows] = fl

    mine = pl.ds(0, ny)
    other = pair[1 - core]
    beyond = across[...]
    before = jnp.where(first_core, beyond, other)
    after = jnp.where(first_core, other, beyond)
    for layer in range(nx):
        describe([before[k, layer] for k in range(3)], layer, mine, layer == nx - 1)
        describe([own[k, layer] for k in range(3)], layer + 2, mine, True)
        describe([after[k, layer] for k in range(3)], layer + 2 + nx, mine, layer == 0)
    above = jnp.where(above_is_even, even[...], odd[...])
    below = jnp.where(above_is_even, odd[...], even[...])
    for layer in range(nx + 2):
        describe([above[k, layer] for k in range(3)], layer + 1, pl.ds(ny, 2), True)
        describe([below[k, layer] for k in range(3)], layer + 1, pl.ds(ny + 2, 2), True)

    col = lax.broadcasted_iota(jnp.int32, (COLS, nz), 0)
    body = (col * 43) >> 8
    mode = col - MODES * body
    bodyf = body.astype(F32)
    lane = lax.broadcasted_iota(jnp.int32, (COLS, nz), 1)
    one = [(mode == m).astype(F32) for m in range(MODES)]
    cen_x = jnp.broadcast_to(cen[:, 0:1], (COLS, nz))
    cen_y = jnp.broadcast_to(cen[:, 1:2], (COLS, nz))
    cen_z = jnp.broadcast_to(cen[:, 2:3], (COLS, nz))
    pos_z = (lane.astype(F32) + 0.5) * (1.0 / nz)
    lever_z = 3.0 * (pos_z - cen_z)
    step3 = one[3] * (3.0 / nz)
    step4 = one[4] * (3.0 / nz)
    coef_x0 = one[0] + one[4] * lever_z
    coef_y0 = one[1] - one[3] * lever_z
    for i in range(ex):
        pos = ((start_x + (i - 2)).astype(F32) + 0.5) / count_x.astype(F32)
        lever = 3.0 * (pos - cen_x)
        cx[0, i] = coef_y0 + one[5] * lever
        cx[1, i] = -one[4] * lever
    for j in range(ey):
        pos = ((start_y + (j if j < ny + 2 else j - ey)).astype(F32) + 0.5) / count_y.astype(F32)
        lever = 3.0 * (pos - cen_y)
        cy[0, j] = coef_x0 - one[5] * lever
        cy[1, j] = one[2] + one[3] * lever

    def at(j):
        return jnp.where(j < 0, j + ey, jnp.where(j >= ey, j - ey, j))

    def row(which, i, j):
        return jnp.broadcast_to(base[which, i, pl.ds(j, 1), :], (COLS, nz))

    def forcing_row(first, i, j, coef_x, coef_y, coef_z):
        value = row(first, i, j) * coef_x + row(first + 1, i, j) * coef_y + row(first + 2, i, j) * coef_z
        return jnp.where(row(first + 3, i, j) == bodyf, value, 0.0)

    def apply(src, i, j, field, along_z):
        beside = src[i + 1, j] + src[i - 1, j]
        beside = beside + src[i, at(j + 1)] + src[i, at(j - 1)]
        beside = beside + along_z
        return field + row(12, i, j) * (5.0 * field - beside)

    for i in range(ex):
        reach = 2 - max(2 - i, i - (nx + 1), 0)

        @pl.loop(-reach, ny + reach)
        def _(j, i=i):
            j = at(j)
            fext[i, j] = forcing_row(0, i, j, cy[0, j], cx[0, i], cy[1, j] + cx[1, i])

    for i in range(1, ex - 1):
        reach = 1 - max(2 - i, i - (nx + 1), 0)

        @pl.loop(-reach, ny + reach)
        def _(j, i=i):
            j = at(j)
            coef_x, coef_y, coef_z = cy[0, j], cx[0, i], cy[1, j] + cx[1, i]
            along_z = forcing_row(4, i, j, coef_x + step4, coef_y - step3, coef_z)
            along_z = along_z + forcing_row(8, i, j, coef_x - step4, coef_y + step3, coef_z)
            qext[i, j] = apply(fext, i, j, fext[i, j], along_z)

    for i in range(2, nx + 2):

        @pl.loop(0, ny, unroll=8)
        def _(j, i=i):
            cells = pl.ds(pl.multiple_of(((i - 2) * ny + j) * nz, nz), nz)
            forcing, field = fext[i, j], qext[i, j]
            up = jnp.where(lane >= 1, pltpu.roll(field, 1, 1), 0.0)
            down = jnp.where(lane < nz - 1, pltpu.roll(field, nz - 1, 1), 0.0)
            lh[0:COLS, cells] = forcing
            lh[COLS : 2 * COLS, cells] = field
            rh[0:COLS, cells] = field
            rh[COLS : 2 * COLS, cells] = apply(qext, i, j, field, up + down)
            fold = forcing[0:FOLD]
            for k in range(1, COLS // FOLD):
                fold = fold + forcing[k * FOLD : (k + 1) * FOLD]
            rh[2 * COLS : 2 * COLS + FOLD, cells] = fold

    grams = dot(lh[...], rh[...], ((1,), (1,)))
    first, second = grams[0:COLS, 0:COLS], grams[COLS : 2 * COLS, 0:COLS]
    third = grams[COLS : 2 * COLS, COLS : 2 * COLS]
    zeroth = grams[0:COLS, 2 * COLS : 2 * COLS + FOLD]
    r = lax.broadcasted_iota(jnp.int32, (COLS, COLS), 0)
    c = lax.broadcasted_iota(jnp.int32, (COLS, COLS), 1)
    diagonal = jnp.sum(jnp.where(r == c, second, 0.0), axis=1, keepdims=True)
    pay[...] = jnp.zeros_like(pay)
    pay[0:COLS, 0:COLS] = jnp.where(r <= c, first, second)
    pay[0:COLS, COLS : COLS + FOLD] = zeroth
    pay[0:COLS, COLS + FOLD : COLS + FOLD + 1] = diagonal
    pay[COLS : 2 * COLS, 0:COLS] = third


def inverse_spd(matrix, work):
    size = matrix.shape[0]
    r = lax.broadcasted_iota(jnp.int32, (size, size), 0)
    c = lax.broadcasted_iota(jnp.int32, (size, size), 1)
    diagonal = jnp.where(r == c, matrix, 0.0)
    scale_r = lax.rsqrt(jnp.sum(diagonal, axis=1, keepdims=True))
    scale_c = lax.rsqrt(jnp.sum(diagonal, axis=0, keepdims=True))
    scaled = matrix * scale_r * scale_c
    bound = jnp.max(jnp.sum(jnp.abs(scaled), axis=0, keepdims=True), axis=1, keepdims=True)
    weight = jnp.minimum(1.0, 1.9 / bound)
    eye = (r == c).astype(F32)
    rest = eye - weight * scaled
    work[0:size] = eye + rest
    work[size : 2 * size] = rest

    def longer(carry):
        power = work[size : 2 * size]
        spread = jnp.sum(power * power)
        total = work[0:size]
        power = mm(power, power)
        total = total + mm(total, power)
        power = mm(power, power)
        work[0:size] = total + mm(total, power)
        work[size : 2 * size] = power
        return carry[0] + 1, spread > 1e-4

    lax.while_loop(lambda carry: (carry[0] < 14) & carry[1], longer, (jnp.int32(0), jnp.bool_(True)))
    return work[0:size] * (weight * scale_r) * scale_c


def solve_kernel(rows, nz, scale, pay, lh, out, added, work):
    r = lax.broadcasted_iota(jnp.int32, (COLS, COLS), 0)
    c = lax.broadcasted_iota(jnp.int32, (COLS, COLS), 1)
    both = pay[0:COLS, 0:COLS]
    both_t = both.T
    third = pay[COLS : 2 * COLS, 0:COLS]
    third = jnp.where(r <= c, third, third.T)
    first = jnp.where(r <= c, both, both_t)
    second = jnp.where(r > c, both, both_t)
    second = jnp.where(r == c, pay[0:COLS, COLS + FOLD : COLS + FOLD + 1], second)
    zeroth = pay[0:COLS, COLS : COLS + FOLD]
    zeroth = jnp.concatenate([zeroth] * (COLS // FOLD), axis=1)
    zeroth = jnp.where(((r * 43) >> 8) == ((c * 43) >> 8), zeroth, 0.0)
    first_inv = inverse_spd(first, work)
    left = mm(first_inv, second)
    right = mm(first_inv, zeroth)
    schur = third - mm(second, left)
    schur = 0.5 * (schur + schur.T)
    later = mm(inverse_spd(schur, work), first - mm(second, right))
    early = right - mm(left, later)
    coeffs = jnp.concatenate([early, later], axis=0)
    values = dot(coeffs, lh[...], ((0,), (0,)))
    added[...] = (mm(zeroth, early) + mm(first, later)) * scale
    for k in range(rows):
        out[pl.ds(k, COLS, stride=rows), :] = values[:, k * nz : (k + 1) * nz]


def swap(array, axes, start):
    size = lax.axis_size(axes)
    pairs = [(i, i + 1) for i in range(start, size - 1, 2)]
    return lax.ppermute(array, axes, pairs + [(j, i) for i, j in pairs])


def reduced(part):
    near, far = (lax.axis_size(axes) for axes in (NEAR, FAR))
    rows, lanes = part.shape
    piece = lax.all_to_all(part, NEAR, 0, 0, tiled=True).reshape(near, rows // near, lanes).sum(0)
    piece = lax.all_to_all(jnp.broadcast_to(piece[None], (far,) + piece.shape), FAR, 0, 0, tiled=True).sum(0)
    return lax.all_to_all(
        jnp.broadcast_to(piece[None], (near,) + piece.shape), NEAR, 0, 0, tiled=True
    ).reshape(rows, lanes)


def shards(surface_tags, normal_index, fluid_mask, body_centers):
    nx, ny, nz = surface_tags.shape
    count_x = nx * lax.axis_size(GX)
    count_y = ny * lax.axis_size(GY)
    at_x, at_y, core = lax.axis_index(GX), lax.axis_index(GY), lax.axis_index("c")
    own = jnp.stack([surface_tags, normal_index, fluid_mask])
    across = swap(own, GX, 1)
    pair = lax.all_gather(own, "c")
    before = jnp.where(core == 0, across, pair[0])[:, nx - 1 :]
    after = jnp.where(core == 0, pair[1], across)[:, :1]
    near = jnp.concatenate([before, own, after], axis=1)
    first, last = near[:, :, :2], near[:, :, ny - 2 :]
    parity = at_y % 2
    odd = swap(jnp.where(parity == 0, first, last), GY, 1)
    even = swap(jnp.where(parity == 0, last, first), GY, 0)
    info = jnp.stack(
        [at_x * nx, at_y * ny, jnp.int32(count_x), jnp.int32(count_y), core, parity]
    ).astype(jnp.int32)
    cen = jnp.repeat(body_centers, MODES, axis=0)
    cells = nx * ny * nz
    vmem = pl.BlockSpec(memory_space=pltpu.VMEM)
    lh, pay = pl.pallas_call(
        functools.partial(fields_kernel, nx, ny, nz),
        out_shape=(
            jax.ShapeDtypeStruct((2 * COLS, cells), F32),
            jax.ShapeDtypeStruct((2 * COLS, 128), F32),
        ),
        in_specs=[pl.BlockSpec(memory_space=pltpu.SMEM)] + [vmem] * 6,
        out_specs=(vmem, vmem),
        scratch_shapes=[
            pltpu.VMEM((2 * COLS + FOLD, cells), F32),
            pltpu.VMEM((13, nx + 4, ny + 4, nz), F32),
            pltpu.VMEM((nx + 4, ny + 4, COLS, nz), F32),
            pltpu.VMEM((nx + 4, ny + 4, COLS, nz), F32),
            pltpu.VMEM((2, nx + 4, COLS, nz), F32),
            pltpu.VMEM((2, ny + 4, COLS, nz), F32),
        ],
        compiler_params=pltpu.CompilerParams(vmem_limit_bytes=40 * 1024 * 1024),
        name="fields",
    )(info, own, pair, across, even, odd, cen)
    pay = reduced(pay)
    scale = 8.0 * BODIES / (count_x * count_y * nz)
    pressure, added = pl.pallas_call(
        functools.partial(solve_kernel, nx * ny, nz, scale),
        out_shape=(
            jax.ShapeDtypeStruct((COLS * nx * ny, nz), F32),
            jax.ShapeDtypeStruct((COLS, COLS), F32),
        ),
        in_specs=[vmem, vmem],
        out_specs=(vmem, vmem),
        scratch_shapes=[pltpu.VMEM((2 * COLS, COLS), F32)],
        compiler_params=pltpu.CompilerParams(vmem_limit_bytes=40 * 1024 * 1024),
        name="solve",
    )(pay, lh)
    return pressure.reshape(COLS, nx, ny, nz), added


def solution(mesh):
    split = Mesh(np.asarray(mesh.devices).reshape(4, 4, 2, 4, 4), GX + GY)
    return jax.shard_map(
        shards,
        mesh=split,
        in_specs=(P(GX, GY, None), P(GX, GY, None), P(GX, GY, None), P()),
        out_specs=(P(None, GX, GY, None), P()),
        check_vma=False,
    )
```

```python
import functools

import jax
import jax.numpy as jnp
import numpy as np
from jax import lax
from jax.experimental import pallas as pl
from jax.experimental.pallas import tpu as pltpu
from jax.sharding import Mesh, PartitionSpec as P

BODIES = 16
MODES = 6
COLS = BODIES * MODES
FOLD = 4 * MODES
GX = ("y", "zh", "c")
GY = ("x", "zl")
NEAR = ("y", "c", "x")
FAR = ("zh", "zl")
F32 = jnp.float32


def dot(left, right, dims):
    return lax.dot_general(
        left, right, (dims, ((), ())), precision=lax.Precision.HIGHEST, preferred_element_type=F32
    )


def mm(left, right):
    return dot(left, right, ((1,), (0,)))


THIRD = COLS // 3


def upper(size):
    r = lax.broadcasted_iota(jnp.int32, (size, size), 0)
    return r <= lax.broadcasted_iota(jnp.int32, (size, size), 1)


def on_diagonal(size):
    r = lax.broadcasted_iota(jnp.int32, (size, size), 0)
    return r == lax.broadcasted_iota(jnp.int32, (size, size), 1)


def chosen(shape, offset):
    r = lax.broadcasted_iota(jnp.int32, shape, 0) - offset
    c = lax.broadcasted_iota(jnp.int32, shape, 1)
    inside = (r >= 0) & (r < FOLD)
    return ((r - c + 2 * COLS) % MODES == 0).astype(F32) * inside.astype(F32)


def shared(left, right):
    size = left.shape[0]
    shape = (size, size + 1)
    r = lax.broadcasted_iota(jnp.int32, shape, 0)
    low = lax.broadcasted_iota(jnp.int32, shape, 1) <= r
    blank = jnp.zeros((size, 1), F32)
    return jnp.where(low, jnp.concatenate([right, blank], axis=1), jnp.concatenate([blank, left], axis=1))


def unshared(both):
    size = both.shape[0]
    left, right = both[:, 1 : size + 1], both[:, 0:size]
    keep = upper(size)
    return jnp.where(keep, left, left.T), jnp.where(keep, right.T, right)


def unpacked(pay):
    t = THIRD
    first, second = unshared(pay[0:COLS, 0 : COLS + 1])
    at = COLS + 1
    r = lax.broadcasted_iota(jnp.int32, (COLS, COLS), 0)
    c = lax.broadcasted_iota(jnp.int32, (COLS, COLS), 1)
    zeroth = mm(pay[0:COLS, at : at + MODES], chosen((MODES, COLS), 0))
    zeroth = jnp.where(((r * 43) >> 8) == ((c * 43) >> 8), zeroth, 0.0)
    at, half = at + MODES, t // 2 + 1
    middle, end = unshared(
        jnp.concatenate([pay[0:t, at : at + half], pay[t : 2 * t, at : at + half - 1]], axis=1)
    )
    block = [pay[COLS : COLS + t, t * k : t * (k + 1)] for k in range(4)]
    third = jnp.concatenate(
        [
            jnp.concatenate([block[3], block[0], block[1]], axis=1),
            jnp.concatenate([block[0].T, middle, block[2]], axis=1),
            jnp.concatenate([block[1].T, block[2].T, end], axis=1),
        ],
        axis=0,
    )
    return zeroth, first, second, third


class Rows:
    def __init__(self, nx, ny, nz, base, cx, cy, fext, qext):
        self.nx, self.ny, self.nz, self.ey = nx, ny, nz, ny + 4
        self.base, self.cx, self.cy, self.fext, self.qext = base, cx, cy, fext, qext
        col = lax.broadcasted_iota(jnp.int32, (COLS, nz), 0)
        body = (col * 43) >> 8
        mode = col - MODES * body
        self.bodyf = body.astype(F32)
        self.one = [(mode == m).astype(F32) for m in range(MODES)]
        self.step3 = self.one[3] * (3.0 / nz)
        self.step4 = self.one[4] * (3.0 / nz)

    def describe(self, cells, layer, rows, shifts):
        nz, base = self.nz, self.base
        lane = lax.broadcasted_iota(jnp.int32, (1, nz), 1)
        tags, index, fluid = cells
        shifted = index + (index >= 13).astype(jnp.int32)
        part_x = (shifted >= 9).astype(jnp.int32) + (shifted >= 18).astype(jnp.int32)
        rest = shifted - 9 * part_x
        part_y = (rest >= 3).astype(jnp.int32) + (rest >= 6).astype(jnp.int32)
        part_z = rest - 3 * part_y
        comps = [(part - 1).astype(F32) for part in (part_x, part_y, part_z)]
        inverse = 1.0 / jnp.sqrt(comps[0] * comps[0] + comps[1] * comps[1] + comps[2] * comps[2])
        fl = fluid.astype(F32)
        values = [comp * inverse * fl for comp in comps] + [tags.astype(F32)]
        for m, value in enumerate(values):
            base[m, layer, rows] = value
            if shifts:
                after = pltpu.roll(value, nz - 1, value.ndim - 1)
                before = pltpu.roll(value, 1, value.ndim - 1)
                if m == 3:
                    after = jnp.where(lane == nz - 1, -1.0, after)
                    before = jnp.where(lane == 0, -1.0, before)
                base[4 + m, layer, rows] = after
                base[8 + m, layer, rows] = before
        base[12, layer, rows] = fl

    def coefficients(self, info, cen):
        nz, one = self.nz, self.one
        start_x, start_y, count_x, count_y = (info[k] for k in range(4))
        column = lax.broadcasted_iota(jnp.int32, (COLS, BODIES), 0)
        mine = ((column * 43) >> 8) == lax.broadcasted_iota(jnp.int32, (COLS, BODIES), 1)
        spread = dot(mine.astype(F32), cen[...], ((1,), (1,)))
        cen_x, cen_y, cen_z = (jnp.broadcast_to(spread[:, d : d + 1], (COLS, nz)) for d in range(3))
        lane = lax.broadcasted_iota(jnp.int32, (COLS, nz), 1)
        lever_z = 3.0 * ((lane.astype(F32) + 0.5) * (1.0 / nz) - cen_z)
        coef_x0 = one[0] + one[4] * lever_z
        coef_y0 = one[1] - one[3] * lever_z
        for i in range(self.nx + 4):
            lever = 3.0 * (((start_x + (i - 2)).astype(F32) + 0.5) / count_x.astype(F32) - cen_x)
            self.cx[0, i] = coef_y0 + one[5] * lever
            self.cx[1, i] = -one[4] * lever
        for j in range(self.ey):
            y = j if j < self.ny + 2 else j - self.ey
            lever = 3.0 * (((start_y + y).astype(F32) + 0.5) / count_y.astype(F32) - cen_y)
            self.cy[0, j] = coef_x0 - one[5] * lever
            self.cy[1, j] = one[2] + one[3] * lever

    def at(self, j):
        return jnp.where(j < 0, j + self.ey, jnp.where(j >= self.ey, j - self.ey, j))

    def row(self, which, i, j):
        return jnp.broadcast_to(self.base[which, i, pl.ds(j, 1), :], (COLS, self.nz))

    def sample(self, first, i, j, coefs):
        value = self.row(first, i, j) * coefs[0]
        value = value + self.row(first + 1, i, j) * coefs[1] + self.row(first + 2, i, j) * coefs[2]
        return jnp.where(self.row(first + 3, i, j) == self.bodyf, value, 0.0)

    def coefs(self, i, j):
        return self.cy[0, j], self.cx[0, i], self.cy[1, j] + self.cx[1, i]

    def forcing(self, i, j):
        j = self.at(j)
        self.fext[i, j] = self.sample(0, i, j, self.coefs(i, j))

    def both(self, i, j):
        j = self.at(j)
        x, y, z = self.coefs(i, j)
        self.fext[i, j] = self.sample(0, i, j, (x, y, z))
        after = self.sample(4, i, j, (x + self.step4, y - self.step3, z))
        self.qext[i, j] = after + self.sample(8, i, j, (x - self.step4, y + self.step3, z))

    def apply(self, src, i, j, field, along_z):
        beside = src[i + 1, j] + src[i - 1, j]
        beside = beside + src[i, self.at(j + 1)] + src[i, self.at(j - 1)]
        beside = beside + along_z
        return field + self.row(12, i, j) * (5.0 * field - beside)

    def operated(self, i, j):
        j = self.at(j)
        self.qext[i, j] = self.apply(self.fext, i, j, self.fext[i, j], self.qext[i, j])

    def collect(self, i, j, cells, lh, rh):
        nz = self.nz
        lane = lax.broadcasted_iota(jnp.int32, (COLS, nz), 1)
        forcing, field = self.fext[i, j], self.qext[i, j]
        up = jnp.where(lane >= 1, pltpu.roll(field, 1, 1), 0.0)
        down = jnp.where(lane < nz - 1, pltpu.roll(field, nz - 1, 1), 0.0)
        lh[0:COLS, cells] = forcing
        lh[COLS : 2 * COLS, cells] = field
        rh[0:COLS, cells] = field
        rh[COLS : 2 * COLS, cells] = self.apply(self.qext, i, j, field, up + down)
        fold = forcing[0:FOLD]
        for k in range(1, COLS // FOLD):
            fold = fold + forcing[k * FOLD : (k + 1) * FOLD]
        rh[2 * COLS : 2 * COLS + FOLD, cells] = fold


    @staticmethod
    def pack(grams, pay):
        first, second = grams[0:COLS, 0:COLS], grams[COLS : 2 * COLS, 0:COLS]
        third = grams[COLS : 2 * COLS, COLS : 2 * COLS]
        t = THIRD
        zeroth = mm(grams[0:COLS, 2 * COLS : 2 * COLS + FOLD], chosen((FOLD, MODES), 0))
        blocks = [[third[t * p : t * (p + 1), t * q : t * (q + 1)] for q in range(3)] for p in range(3)]
        ends = shared(blocks[1][1], blocks[2][2])
        half = t // 2 + 1
        ends = jnp.concatenate([ends[:, :half], jnp.pad(ends[:, half:], ((0, t), (0, 1)))], axis=0)
        unused = jnp.zeros((COLS, 128 - COLS - 1 - MODES - half), F32)
        pay[0:COLS, :] = jnp.concatenate([shared(first, second), zeroth, ends, unused], axis=1)
        pay[COLS : COLS + t, :] = jnp.concatenate([blocks[0][1], blocks[0][2], blocks[1][2], blocks[0][0]], axis=1)


def own_kernel(nx, ny, nz, info, own, cen_hbm, base, cx, cy, fext, qext, cen, sem):
    centers = pltpu.make_async_copy(cen_hbm, cen, sem)
    centers.start()
    rows = Rows(nx, ny, nz, base, cx, cy, fext, qext)
    for layer in range(nx):
        rows.describe([own[k, layer] for k in range(3)], layer + 2, pl.ds(0, ny), True)
    centers.wait()
    rows.coefficients(info, cen)
    for i in range(2, nx + 2):

        @pl.loop(0, ny, unroll=True)
        def _(j, i=i):
            rows.both(i, j)


def inner_kernel(nx, ny, nz, info, across, pair, cx, cy, base_in, fext_in, qext_in, base, fext, qext, lh, gram, rh):
    del base_in, fext_in, qext_in
    rows = Rows(nx, ny, nz, base, cx, cy, fext, qext)
    core = info[4]
    other, beyond = pair[...], across[...]
    before = jnp.where(core == 0, beyond, other)
    after = jnp.where(core == 0, other, beyond)
    for layer in range(nx):
        rows.describe([before[k, layer] for k in range(3)], layer, pl.ds(0, ny), layer == nx - 1)
        rows.describe([after[k, layer] for k in range(3)], layer + 2 + nx, pl.ds(0, ny), layer == 0)
    for i in (0, 1, nx + 2, nx + 3):

        @pl.loop(0, ny, unroll=True)
        def _(j, i=i):
            if i in (1, nx + 2):
                rows.both(i, j)
            else:
                rows.forcing(i, j)

    for i in range(1, nx + 3):

        @pl.loop(1, ny - 1, unroll=True)
        def _(j, i=i):
            rows.operated(i, j)

    for i in range(2, nx + 2):

        @pl.loop(0, ny - 4, unroll=True)
        def _(k, i=i):
            cells = pl.ds(pl.multiple_of(((i - 2) * (ny - 4) + k) * nz, nz), nz)
            rows.collect(i, k + 2, cells, lh, rh)

    gram[...] = dot(lh[...], rh[...], ((1,), (1,)))


def outer_kernel(
    nx, ny, nz, info, odd, even, cx, cy, base_in, fext_in, qext_in, gram, base, fext, qext, lh, pay, rh
):
    del base_in, fext_in, qext_in
    rows = Rows(nx, ny, nz, base, cx, cy, fext, qext)
    parity = info[5]
    above = jnp.where(parity == 0, even[...], odd[...])
    below = jnp.where(parity == 0, odd[...], even[...])
    for layer in range(nx + 2):
        rows.describe([above[k, layer] for k in range(3)], layer + 1, pl.ds(ny, 2), True)
        rows.describe([below[k, layer] for k in range(3)], layer + 1, pl.ds(ny + 2, 2), True)
    for i in range(1, nx + 3):
        reach = 2 if 2 <= i < nx + 2 else 1
        for j in list(range(-reach, 0)) + list(range(ny, ny + reach)):
            if j in (-1, ny) and 2 <= i < nx + 2:
                rows.both(i, j)
            else:
                rows.forcing(i, j)
    for i in range(1, nx + 3):
        inside = 2 <= i < nx + 2

        @pl.loop(0, 2, unroll=True)
        def _(k, i=i):
            rows.operated(i, k * (ny - 1))

        if inside:

            @pl.loop(0, 2, unroll=True)
            def _(k, i=i):
                rows.operated(i, k * (ny + 1) - 1)

    for i in range(2, nx + 2):

        @pl.loop(0, 4, unroll=True)
        def _(k, i=i):
            cells = pl.ds(pl.multiple_of(((i - 2) * 4 + k) * nz, nz), nz)
            rows.collect(i, jnp.where(k < 2, k, k + ny - 4), cells, lh, rh)

    rows.pack(gram[...] + dot(lh[...], rh[...], ((1,), (1,))), pay)


def inverse_spd(matrix, work):
    size = matrix.shape[0]
    r = lax.broadcasted_iota(jnp.int32, (size, size), 0)
    c = lax.broadcasted_iota(jnp.int32, (size, size), 1)
    diagonal = jnp.where(r == c, matrix, 0.0)
    scale_r = lax.rsqrt(jnp.sum(diagonal, axis=1, keepdims=True))
    scale_c = lax.rsqrt(jnp.sum(diagonal, axis=0, keepdims=True))
    scaled = matrix * scale_r * scale_c
    square = mm(scaled, scaled)
    bound = jnp.max(jnp.sum(jnp.abs(square), axis=0, keepdims=True), axis=1, keepdims=True)
    weight = jnp.minimum(1.0, 1.9 * lax.rsqrt(bound))
    eye = (r == c).astype(F32)
    twice = 2.0 * eye - weight * scaled
    work[0:size] = twice
    work[size : 2 * size] = twice - eye - weight * (scaled - weight * square)

    def longer(carry):
        power = work[size : 2 * size]
        more = mm(work[...], power)
        work[0:size] = work[0:size] + more[:size]
        work[size : 2 * size] = more[size:]
        return carry[0] + 1, jnp.sum(power * power) > 3e-7

    lax.while_loop(lambda carry: (carry[0] < 28) & carry[1], longer, (jnp.int32(0), jnp.bool_(True)))
    return work[0:size] * (weight * scale_r) * scale_c


def solve_kernel(nx, ny, nz, scale, pay, inner, outer, out, added, work):
    zeroth, first, second, third = unpacked(pay)
    center = jnp.where(on_diagonal(COLS), second / first, 0.0)
    shift = jnp.sum(jnp.sum(center, axis=1, keepdims=True), axis=0, keepdims=True) * (1.0 / COLS)
    cross = second - shift * first
    energy = jnp.concatenate(
        [
            jnp.concatenate([first, cross], axis=1),
            jnp.concatenate([cross, third - shift * (second + cross)], axis=1),
        ],
        axis=0,
    )
    solved = mm(inverse_spd(energy, work), jnp.concatenate([zeroth, first - shift * zeroth], axis=0))
    later = solved[COLS:]
    early = solved[:COLS] - shift * later
    coeffs = jnp.concatenate([early, later], axis=0)
    rows = nx * ny
    for lh, places in ((inner, range(2, ny - 2)), (outer, [0, 1, ny - 2, ny - 1])):
        values = dot(coeffs, lh[...], ((0,), (0,)))
        for k, (i, j) in enumerate((i, j) for i in range(nx) for j in places):
            out[pl.ds(i * ny + j, COLS, stride=rows), :] = values[:, k * nz : (k + 1) * nz]
    added[...] = (mm(zeroth, early) + mm(first, later)) * scale


def swap(array, axes, start):
    size = lax.axis_size(axes)
    pairs = [(i, i + 1) for i in range(start, size - 1, 2)]
    return lax.ppermute(array, axes, pairs + [(j, i) for i, j in pairs])


def reduced(part):
    near, far = (lax.axis_size(axes) for axes in (NEAR, FAR))
    rows, lanes = part.shape
    piece = lax.all_to_all(part, NEAR, 0, 0, tiled=True).reshape(near, rows // near, lanes).sum(0)
    piece = lax.all_to_all(jnp.broadcast_to(piece[None], (far,) + piece.shape), FAR, 0, 0, tiled=True).sum(0)
    return lax.all_to_all(
        jnp.broadcast_to(piece[None], (near,) + piece.shape), NEAR, 0, 0, tiled=True
    ).reshape(rows, lanes)


def shards(surface_tags, normal_index, fluid_mask, body_centers):
    nx, ny, nz = surface_tags.shape
    count_x = nx * lax.axis_size(GX)
    count_y = ny * lax.axis_size(GY)
    at_x, at_y, core = lax.axis_index(GX), lax.axis_index(GY), lax.axis_index("c")
    own = lax.optimization_barrier(jnp.stack([surface_tags, normal_index, fluid_mask]))
    across = swap(own, GX, 1)
    pair = lax.ppermute(own, "c", [(0, 1), (1, 0)])
    before = jnp.where(core == 1, pair, across)[:, nx - 1 :]
    after = jnp.where(core == 0, pair, across)[:, :1]
    near = jnp.concatenate([before, own, after], axis=1)
    first, last = near[:, :, :2], near[:, :, ny - 2 :]
    parity = at_y % 2
    even = swap(jnp.where(parity == 0, last, first), GY, 0)
    odd = swap(jnp.where(parity == 0, first, last), GY, 1)
    info = jnp.stack(
        [at_x * nx, at_y * ny, jnp.int32(count_x), jnp.int32(count_y), core, parity]
    ).astype(jnp.int32)
    half = nx * ny * nz // 2
    ex, ey = nx + 4, ny + 4
    vmem = pl.BlockSpec(memory_space=pltpu.VMEM)
    smem = pl.BlockSpec(memory_space=pltpu.SMEM)

    def shape(*dims):
        return jax.ShapeDtypeStruct(dims, F32)

    def call(kernel, outs, ins, scratch, flops, aliases, name, last=vmem):
        return pl.pallas_call(
            functools.partial(kernel, nx, ny, nz),
            out_shape=outs,
            in_specs=[smem] + [vmem] * (len(ins) - 2) + [last],
            out_specs=tuple(vmem for _ in outs),
            scratch_shapes=scratch,
            input_output_aliases=aliases,
            compiler_params=pltpu.CompilerParams(vmem_limit_bytes=24 * 1024 * 1024),
            cost_estimate=pl.CostEstimate(flops=flops, bytes_accessed=8 * 1024 * 1024, transcendentals=0),
            name=name,
        )(*ins)

    base, field = shape(13, ex, ey, nz), shape(ex, ey, COLS, nz)
    base, cx, cy, fext, qext = call(
        own_kernel, (base, shape(2, ex, COLS, nz), shape(2, ey, COLS, nz), field, field),
        (info, own, body_centers.T), [pltpu.VMEM((3, BODIES), F32), pltpu.SemaphoreType.DMA], 1 << 28, {}, "own_rows",
        pl.BlockSpec(memory_space=pltpu.HBM),
    )
    rh = [pltpu.VMEM((2 * COLS + FOLD, half), F32)]
    base, fext, qext, inner, gram = call(
        inner_kernel,
        (shape(*base.shape), shape(*fext.shape), shape(*qext.shape), shape(2 * COLS, half), shape(2 * COLS, 2 * COLS + FOLD)),
        (info, across, pair, cx, cy, base, fext, qext), rh, 1 << 29, {5: 0, 6: 1, 7: 2}, "inner_rows",
    )
    _, _, _, outer, pay = call(
        outer_kernel,
        (shape(*base.shape), shape(*fext.shape), shape(*qext.shape), shape(2 * COLS, half), shape(COLS + THIRD, 128)),
        (info, odd, even, cx, cy, base, fext, qext, gram), rh, 1 << 29, {5: 0, 6: 1, 7: 2}, "outer_rows",
    )
    pay = reduced(pay)
    scale = 8.0 * BODIES / (count_x * count_y * nz)
    pressure, added = pl.pallas_call(
        functools.partial(solve_kernel, nx, ny, nz, scale),
        out_shape=(
            jax.ShapeDtypeStruct((COLS * nx * ny, nz), F32),
            jax.ShapeDtypeStruct((COLS, COLS), F32),
        ),
        in_specs=[vmem] * 3,
        out_specs=(vmem, vmem),
        scratch_shapes=[pltpu.VMEM((4 * COLS, 2 * COLS), F32)],
        compiler_params=pltpu.CompilerParams(vmem_limit_bytes=24 * 1024 * 1024),
        name="solve",
    )(pay, inner, outer)
    return pressure.reshape(COLS, nx, ny, nz), added


def solution(mesh):
    split = Mesh(np.asarray(mesh.devices).reshape(4, 4, 2, 4, 4), GX + GY)
    return jax.shard_map(
        shards,
        mesh=split,
        in_specs=(P(GX, GY, None), P(GX, GY, None), P(GX, GY, None), P()),
        out_specs=(P(None, GX, GY, None), P()),
        check_vma=False,
    )
```

```python
import functools

import jax
import jax.numpy as jnp
import numpy as np
from jax import lax
from jax.experimental import pallas as pl
from jax.experimental.pallas import tpu as pltpu
from jax.sharding import Mesh, PartitionSpec as P

BODIES = 16
MODES = 6
COLS = BODIES * MODES
FOLD = 4 * MODES
GX = ("y", "zh", "c")
GY = ("x", "zl")
NEAR = ("y", "c", "x")
FAR = ("zh", "zl")
F32 = jnp.float32


def dot(left, right, dims):
    return lax.dot_general(
        left, right, (dims, ((), ())), precision=lax.Precision.HIGHEST, preferred_element_type=F32
    )


def mm(left, right):
    return dot(left, right, ((1,), (0,)))


THIRD = COLS // 3


def upper(size):
    r = lax.broadcasted_iota(jnp.int32, (size, size), 0)
    return r <= lax.broadcasted_iota(jnp.int32, (size, size), 1)


def on_diagonal(size):
    r = lax.broadcasted_iota(jnp.int32, (size, size), 0)
    return r == lax.broadcasted_iota(jnp.int32, (size, size), 1)


def chosen(shape, offset):
    r = lax.broadcasted_iota(jnp.int32, shape, 0) - offset
    c = lax.broadcasted_iota(jnp.int32, shape, 1)
    inside = (r >= 0) & (r < FOLD)
    return ((r - c + 2 * COLS) % MODES == 0).astype(F32) * inside.astype(F32)


def shared(left, right):
    size = left.shape[0]
    shape = (size, size + 1)
    r = lax.broadcasted_iota(jnp.int32, shape, 0)
    low = lax.broadcasted_iota(jnp.int32, shape, 1) <= r
    blank = jnp.zeros((size, 1), F32)
    return jnp.where(low, jnp.concatenate([right, blank], axis=1), jnp.concatenate([blank, left], axis=1))


def unshared(both):
    size = both.shape[0]
    left, right = both[:, 1 : size + 1], both[:, 0:size]
    keep = upper(size)
    return jnp.where(keep, left, left.T), jnp.where(keep, right.T, right)


def unpacked(pay):
    t = THIRD
    first, second = unshared(pay[0:COLS, 0 : COLS + 1])
    at = COLS + 1
    r = lax.broadcasted_iota(jnp.int32, (COLS, COLS), 0)
    c = lax.broadcasted_iota(jnp.int32, (COLS, COLS), 1)
    zeroth = mm(pay[0:COLS, at : at + MODES], chosen((MODES, COLS), 0))
    zeroth = jnp.where(((r * 43) >> 8) == ((c * 43) >> 8), zeroth, 0.0)
    at, half = at + MODES, t // 2 + 1
    middle, end = unshared(
        jnp.concatenate([pay[0:t, at : at + half], pay[t : 2 * t, at : at + half - 1]], axis=1)
    )
    block = [pay[COLS : COLS + t, t * k : t * (k + 1)] for k in range(4)]
    third = jnp.concatenate(
        [
            jnp.concatenate([block[3], block[0], block[1]], axis=1),
            jnp.concatenate([block[0].T, middle, block[2]], axis=1),
            jnp.concatenate([block[1].T, block[2].T, end], axis=1),
        ],
        axis=0,
    )
    return zeroth, first, second, third


class Rows:
    def __init__(self, nx, ny, nz, base, cx, cy, fext, qext):
        self.nx, self.ny, self.nz, self.ey = nx, ny, nz, ny + 4
        self.base, self.cx, self.cy, self.fext, self.qext = base, cx, cy, fext, qext
        col = lax.broadcasted_iota(jnp.int32, (COLS, nz), 0)
        body = (col * 43) >> 8
        mode = col - MODES * body
        self.bodyf = body.astype(F32)
        self.one = [(mode == m).astype(F32) for m in range(MODES)]
        self.step3 = self.one[3] * (3.0 / nz)
        self.step4 = self.one[4] * (3.0 / nz)

    def describe(self, cells, layer, rows, shifts):
        nz, base = self.nz, self.base
        lane = lax.broadcasted_iota(jnp.int32, (1, nz), 1)
        tags, index, fluid = cells
        shifted = index + (index >= 13).astype(jnp.int32)
        part_x = (shifted >= 9).astype(jnp.int32) + (shifted >= 18).astype(jnp.int32)
        rest = shifted - 9 * part_x
        part_y = (rest >= 3).astype(jnp.int32) + (rest >= 6).astype(jnp.int32)
        part_z = rest - 3 * part_y
        comps = [(part - 1).astype(F32) for part in (part_x, part_y, part_z)]
        inverse = 1.0 / jnp.sqrt(comps[0] * comps[0] + comps[1] * comps[1] + comps[2] * comps[2])
        fl = fluid.astype(F32)
        values = [comp * inverse * fl for comp in comps] + [tags.astype(F32)]
        for m, value in enumerate(values):
            base[m, layer, rows] = value
            if shifts:
                after = pltpu.roll(value, nz - 1, value.ndim - 1)
                before = pltpu.roll(value, 1, value.ndim - 1)
                if m == 3:
                    after = jnp.where(lane == nz - 1, -1.0, after)
                    before = jnp.where(lane == 0, -1.0, before)
                base[4 + m, layer, rows] = after
                base[8 + m, layer, rows] = before
        base[12, layer, rows] = fl

    def coefficients(self, info, cen):
        nz, one = self.nz, self.one
        start_x, start_y, count_x, count_y = (info[k] for k in range(4))
        column = lax.broadcasted_iota(jnp.int32, (COLS, BODIES), 0)
        mine = ((column * 43) >> 8) == lax.broadcasted_iota(jnp.int32, (COLS, BODIES), 1)
        spread = dot(mine.astype(F32), cen[...], ((1,), (1,)))
        cen_x, cen_y, cen_z = (jnp.broadcast_to(spread[:, d : d + 1], (COLS, nz)) for d in range(3))
        lane = lax.broadcasted_iota(jnp.int32, (COLS, nz), 1)
        lever_z = 3.0 * ((lane.astype(F32) + 0.5) * (1.0 / nz) - cen_z)
        coef_x0 = one[0] + one[4] * lever_z
        coef_y0 = one[1] - one[3] * lever_z
        for i in range(self.nx + 4):
            lever = 3.0 * (((start_x + (i - 2)).astype(F32) + 0.5) / count_x.astype(F32) - cen_x)
            self.cx[0, i] = coef_y0 + one[5] * lever
            self.cx[1, i] = -one[4] * lever
        for j in range(self.ey):
            y = j if j < self.ny + 2 else j - self.ey
            lever = 3.0 * (((start_y + y).astype(F32) + 0.5) / count_y.astype(F32) - cen_y)
            self.cy[0, j] = coef_x0 - one[5] * lever
            self.cy[1, j] = one[2] + one[3] * lever

    def at(self, j):
        return jnp.where(j < 0, j + self.ey, jnp.where(j >= self.ey, j - self.ey, j))

    def row(self, which, i, j):
        return jnp.broadcast_to(self.base[which, i, pl.ds(j, 1), :], (COLS, self.nz))

    def sample(self, first, i, j, coefs):
        value = self.row(first, i, j) * coefs[0]
        value = value + self.row(first + 1, i, j) * coefs[1] + self.row(first + 2, i, j) * coefs[2]
        return jnp.where(self.row(first + 3, i, j) == self.bodyf, value, 0.0)

    def coefs(self, i, j):
        return self.cy[0, j], self.cx[0, i], self.cy[1, j] + self.cx[1, i]

    def forcing(self, i, j):
        j = self.at(j)
        self.fext[i, j] = self.sample(0, i, j, self.coefs(i, j))

    def both(self, i, j):
        j = self.at(j)
        x, y, z = self.coefs(i, j)
        self.fext[i, j] = self.sample(0, i, j, (x, y, z))
        after = self.sample(4, i, j, (x + self.step4, y - self.step3, z))
        self.qext[i, j] = after + self.sample(8, i, j, (x - self.step4, y + self.step3, z))

    def apply(self, src, i, j, field, along_z):
        beside = src[i + 1, j] + src[i - 1, j]
        beside = beside + src[i, self.at(j + 1)] + src[i, self.at(j - 1)]
        beside = beside + along_z
        return field + self.row(12, i, j) * (5.0 * field - beside)

    def operated(self, i, j):
        j = self.at(j)
        self.qext[i, j] = self.apply(self.fext, i, j, self.fext[i, j], self.qext[i, j])

    def collect(self, i, j, cells, lh, rh):
        nz = self.nz
        lane = lax.broadcasted_iota(jnp.int32, (COLS, nz), 1)
        forcing, field = self.fext[i, j], self.qext[i, j]
        up = jnp.where(lane >= 1, pltpu.roll(field, 1, 1), 0.0)
        down = jnp.where(lane < nz - 1, pltpu.roll(field, nz - 1, 1), 0.0)
        lh[0:COLS, cells] = forcing
        lh[COLS : 2 * COLS, cells] = field
        rh[0:COLS, cells] = field
        rh[COLS : 2 * COLS, cells] = self.apply(self.qext, i, j, field, up + down)
        fold = forcing[0:FOLD]
        for k in range(1, COLS // FOLD):
            fold = fold + forcing[k * FOLD : (k + 1) * FOLD]
        rh[2 * COLS : 2 * COLS + FOLD, cells] = fold


    @staticmethod
    def pack(grams, pay):
        first, second = grams[0:COLS, 0:COLS], grams[COLS : 2 * COLS, 0:COLS]
        third = grams[COLS : 2 * COLS, COLS : 2 * COLS]
        t = THIRD
        zeroth = mm(grams[0:COLS, 2 * COLS : 2 * COLS + FOLD], chosen((FOLD, MODES), 0))
        blocks = [[third[t * p : t * (p + 1), t * q : t * (q + 1)] for q in range(3)] for p in range(3)]
        ends = shared(blocks[1][1], blocks[2][2])
        half = t // 2 + 1
        ends = jnp.concatenate([ends[:, :half], jnp.pad(ends[:, half:], ((0, t), (0, 1)))], axis=0)
        unused = jnp.zeros((COLS, 128 - COLS - 1 - MODES - half), F32)
        pay[0:COLS, :] = jnp.concatenate([shared(first, second), zeroth, ends, unused], axis=1)
        pay[COLS : COLS + t, :] = jnp.concatenate([blocks[0][1], blocks[0][2], blocks[1][2], blocks[0][0]], axis=1)


def own_kernel(nx, ny, nz, info, own, cen_hbm, base, cx, cy, fext, qext, cen, sem):
    centers = pltpu.make_async_copy(cen_hbm, cen, sem)
    centers.start()
    rows = Rows(nx, ny, nz, base, cx, cy, fext, qext)
    for layer in range(nx):
        rows.describe([own[k, layer] for k in range(3)], layer + 2, pl.ds(0, ny), True)
    centers.wait()
    rows.coefficients(info, cen)
    for i in range(2, nx + 2):

        @pl.loop(0, ny, unroll=True)
        def _(j, i=i):
            rows.both(i, j)


def inner_kernel(nx, ny, nz, info, across, pair, cx, cy, base_in, fext_in, qext_in, base, fext, qext, lh, gram, rh):
    del base_in, fext_in, qext_in
    rows = Rows(nx, ny, nz, base, cx, cy, fext, qext)
    core = info[4]
    other, beyond = pair[...], across[...]
    before = jnp.where(core == 0, beyond, other)
    after = jnp.where(core == 0, other, beyond)
    for layer in range(nx):
        rows.describe([before[k, layer] for k in range(3)], layer, pl.ds(0, ny), layer == nx - 1)
        rows.describe([after[k, layer] for k in range(3)], layer + 2 + nx, pl.ds(0, ny), layer == 0)
    for i in (0, 1, nx + 2, nx + 3):

        @pl.loop(0, ny, unroll=True)
        def _(j, i=i):
            if i in (1, nx + 2):
                rows.both(i, j)
            else:
                rows.forcing(i, j)

    for i in range(1, nx + 3):

        @pl.loop(1, ny - 1, unroll=True)
        def _(j, i=i):
            rows.operated(i, j)

    for i in range(2, nx + 2):

        @pl.loop(0, ny - 4, unroll=True)
        def _(k, i=i):
            cells = pl.ds(pl.multiple_of(((i - 2) * (ny - 4) + k) * nz, nz), nz)
            rows.collect(i, k + 2, cells, lh, rh)

    gram[...] = dot(lh[...], rh[...], ((1,), (1,)))


def outer_kernel(
    nx, ny, nz, info, odd, even, cx, cy, base_in, fext_in, qext_in, gram, base, fext, qext, lh, pay, rh
):
    del base_in, fext_in, qext_in
    rows = Rows(nx, ny, nz, base, cx, cy, fext, qext)
    parity = info[5]
    above = jnp.where(parity == 0, even[...], odd[...])
    below = jnp.where(parity == 0, odd[...], even[...])
    for layer in range(nx + 2):
        rows.describe([above[k, layer] for k in range(3)], layer + 1, pl.ds(ny, 2), True)
        rows.describe([below[k, layer] for k in range(3)], layer + 1, pl.ds(ny + 2, 2), True)
    for i in range(1, nx + 3):
        reach = 2 if 2 <= i < nx + 2 else 1
        for j in list(range(-reach, 0)) + list(range(ny, ny + reach)):
            if j in (-1, ny) and 2 <= i < nx + 2:
                rows.both(i, j)
            else:
                rows.forcing(i, j)
    for i in range(1, nx + 3):
        inside = 2 <= i < nx + 2

        @pl.loop(0, 2, unroll=True)
        def _(k, i=i):
            rows.operated(i, k * (ny - 1))

        if inside:

            @pl.loop(0, 2, unroll=True)
            def _(k, i=i):
                rows.operated(i, k * (ny + 1) - 1)

    for i in range(2, nx + 2):

        @pl.loop(0, 4, unroll=True)
        def _(k, i=i):
            cells = pl.ds(pl.multiple_of(((i - 2) * 4 + k) * nz, nz), nz)
            rows.collect(i, jnp.where(k < 2, k, k + ny - 4), cells, lh, rh)

    rows.pack(gram[...] + dot(lh[...], rh[...], ((1,), (1,))), pay)


def inverse_spd(matrix, work):
    size = matrix.shape[0]
    r = lax.broadcasted_iota(jnp.int32, (size, size), 0)
    c = lax.broadcasted_iota(jnp.int32, (size, size), 1)
    diagonal = jnp.where(r == c, matrix, 0.0)
    scale_r = lax.rsqrt(jnp.sum(diagonal, axis=1, keepdims=True))
    scale_c = lax.rsqrt(jnp.sum(diagonal, axis=0, keepdims=True))
    scaled = matrix * scale_r * scale_c
    square = mm(scaled, scaled)
    bound = jnp.max(jnp.sum(jnp.abs(square), axis=0, keepdims=True), axis=1, keepdims=True)
    weight = lax.rsqrt(bound)
    eye = (r == c).astype(F32)
    work[0:size] = (30.0 / 7.0) * eye - (25.0 / 7.0 * weight) * scaled
    work[size : 2 * size] = eye - (30.0 / 7.0 * weight) * scaled + (25.0 / 7.0 * weight * weight) * square

    def longer(carry):
        power = work[size : 2 * size]
        more = mm(work[...], power)
        work[0:size] = work[0:size] + more[:size]
        work[size : 2 * size] = more[size:]
        return carry[0] + 1, jnp.sum(power * power) > 2e-6

    lax.while_loop(lambda carry: (carry[0] < 28) & carry[1], longer, (jnp.int32(0), jnp.bool_(True)))
    return work[0:size] * (weight * scale_r) * scale_c


def solve_kernel(nx, ny, nz, scale, pay, inner, outer, out, added, work):
    zeroth, first, second, third = unpacked(pay)
    center = jnp.where(on_diagonal(COLS), second / first, 0.0)
    shift = jnp.sum(jnp.sum(center, axis=1, keepdims=True), axis=0, keepdims=True) * (1.0 / COLS)
    cross = second - shift * first
    energy = jnp.concatenate(
        [
            jnp.concatenate([first, cross], axis=1),
            jnp.concatenate([cross, third - shift * (second + cross)], axis=1),
        ],
        axis=0,
    )
    solved = mm(inverse_spd(energy, work), jnp.concatenate([zeroth, first - shift * zeroth], axis=0))
    later = solved[COLS:]
    early = solved[:COLS] - shift * later
    coeffs = jnp.concatenate([early, later], axis=0)
    rows = nx * ny
    for lh, places in ((inner, range(2, ny - 2)), (outer, [0, 1, ny - 2, ny - 1])):
        values = dot(coeffs, lh[...], ((0,), (0,)))
        for k, (i, j) in enumerate((i, j) for i in range(nx) for j in places):
            out[pl.ds(i * ny + j, COLS, stride=rows), :] = values[:, k * nz : (k + 1) * nz]
    added[...] = (mm(zeroth, early) + mm(first, later)) * scale


def swap(array, axes, start):
    size = lax.axis_size(axes)
    pairs = [(i, i + 1) for i in range(start, size - 1, 2)]
    return lax.ppermute(array, axes, pairs + [(j, i) for i, j in pairs])


def reduced(part):
    near, far = (lax.axis_size(axes) for axes in (NEAR, FAR))
    rows, lanes = part.shape
    piece = lax.all_to_all(part, NEAR, 0, 0, tiled=True).reshape(near, rows // near, lanes).sum(0)
    piece = lax.all_to_all(jnp.broadcast_to(piece[None], (far,) + piece.shape), FAR, 0, 0, tiled=True).sum(0)
    return lax.all_to_all(
        jnp.broadcast_to(piece[None], (near,) + piece.shape), NEAR, 0, 0, tiled=True
    ).reshape(rows, lanes)


def shards(surface_tags, normal_index, fluid_mask, body_centers):
    nx, ny, nz = surface_tags.shape
    count_x = nx * lax.axis_size(GX)
    count_y = ny * lax.axis_size(GY)
    at_x, at_y, core = lax.axis_index(GX), lax.axis_index(GY), lax.axis_index("c")
    own = lax.optimization_barrier(jnp.stack([surface_tags, normal_index, fluid_mask]))
    across = swap(own, GX, 1)
    pair = lax.ppermute(own, "c", [(0, 1), (1, 0)])
    before = jnp.where(core == 1, pair, across)[:, nx - 1 :]
    after = jnp.where(core == 0, pair, across)[:, :1]
    near = jnp.concatenate([before, own, after], axis=1)
    first, last = near[:, :, :2], near[:, :, ny - 2 :]
    parity = at_y % 2
    even = swap(jnp.where(parity == 0, last, first), GY, 0)
    odd = swap(jnp.where(parity == 0, first, last), GY, 1)
    info = jnp.stack(
        [at_x * nx, at_y * ny, jnp.int32(count_x), jnp.int32(count_y), core, parity]
    ).astype(jnp.int32)
    half = nx * ny * nz // 2
    ex, ey = nx + 4, ny + 4
    vmem = pl.BlockSpec(memory_space=pltpu.VMEM)
    smem = pl.BlockSpec(memory_space=pltpu.SMEM)

    def shape(*dims):
        return jax.ShapeDtypeStruct(dims, F32)

    def call(kernel, outs, ins, scratch, flops, aliases, name, last=vmem):
        return pl.pallas_call(
            functools.partial(kernel, nx, ny, nz),
            out_shape=outs,
            in_specs=[smem] + [vmem] * (len(ins) - 2) + [last],
            out_specs=tuple(vmem for _ in outs),
            scratch_shapes=scratch,
            input_output_aliases=aliases,
            compiler_params=pltpu.CompilerParams(vmem_limit_bytes=24 * 1024 * 1024),
            cost_estimate=pl.CostEstimate(flops=flops, bytes_accessed=8 * 1024 * 1024, transcendentals=0),
            name=name,
        )(*ins)

    base, field = shape(13, ex, ey, nz), shape(ex, ey, COLS, nz)
    base, cx, cy, fext, qext = call(
        own_kernel, (base, shape(2, ex, COLS, nz), shape(2, ey, COLS, nz), field, field),
        (info, own, body_centers.T), [pltpu.VMEM((3, BODIES), F32), pltpu.SemaphoreType.DMA], 1 << 28, {}, "own_rows",
        pl.BlockSpec(memory_space=pltpu.HBM),
    )
    rh = [pltpu.VMEM((2 * COLS + FOLD, half), F32)]
    base, fext, qext, inner, gram = call(
        inner_kernel,
        (shape(*base.shape), shape(*fext.shape), shape(*qext.shape), shape(2 * COLS, half), shape(2 * COLS, 2 * COLS + FOLD)),
        (info, across, pair, cx, cy, base, fext, qext), rh, 1 << 29, {5: 0, 6: 1, 7: 2}, "inner_rows",
    )
    _, _, _, outer, pay = call(
        outer_kernel,
        (shape(*base.shape), shape(*fext.shape), shape(*qext.shape), shape(2 * COLS, half), shape(COLS + THIRD, 128)),
        (info, odd, even, cx, cy, base, fext, qext, gram), rh, 1 << 29, {5: 0, 6: 1, 7: 2}, "outer_rows",
    )
    pay = reduced(pay)
    scale = 8.0 * BODIES / (count_x * count_y * nz)
    pressure, added = pl.pallas_call(
        functools.partial(solve_kernel, nx, ny, nz, scale),
        out_shape=(
            jax.ShapeDtypeStruct((COLS * nx * ny, nz), F32),
            jax.ShapeDtypeStruct((COLS, COLS), F32),
        ),
        in_specs=[vmem] * 3,
        out_specs=(vmem, vmem),
        scratch_shapes=[pltpu.VMEM((4 * COLS, 2 * COLS), F32)],
        compiler_params=pltpu.CompilerParams(vmem_limit_bytes=24 * 1024 * 1024),
        name="solve",
    )(pay, inner, outer)
    return pressure.reshape(COLS, nx, ny, nz), added


def solution(mesh):
    split = Mesh(np.asarray(mesh.devices).reshape(4, 4, 2, 4, 4), GX + GY)
    return jax.shard_map(
        shards,
        mesh=split,
        in_specs=(P(GX, GY, None), P(GX, GY, None), P(GX, GY, None), P()),
        out_specs=(P(None, GX, GY, None), P()),
        check_vma=False,
    )
```

```python
import functools

import jax
import jax.numpy as jnp
import numpy as np
from jax import lax
from jax.experimental import pallas as pl
from jax.experimental.pallas import tpu as pltpu
from jax.sharding import Mesh, PartitionSpec as P

BODIES = 16
MODES = 6
COLS = BODIES * MODES
FOLD = 4 * MODES
GX = ("y", "zh", "c")
GY = ("x", "zl")
NEAR = ("y", "c", "x")
FAR = ("zh", "zl")
F32 = jnp.float32


def dot(left, right, dims):
    return lax.dot_general(
        left, right, (dims, ((), ())), precision=lax.Precision.HIGHEST, preferred_element_type=F32
    )


def mm(left, right):
    return dot(left, right, ((1,), (0,)))


THIRD = COLS // 3
NEXT = MODES + 1
PREVIOUS = 2 * NEXT
MASK = 3 * NEXT


def upper(size):
    r = lax.broadcasted_iota(jnp.int32, (size, size), 0)
    return r <= lax.broadcasted_iota(jnp.int32, (size, size), 1)


def on_diagonal(size):
    r = lax.broadcasted_iota(jnp.int32, (size, size), 0)
    return r == lax.broadcasted_iota(jnp.int32, (size, size), 1)


def chosen(shape, offset):
    r = lax.broadcasted_iota(jnp.int32, shape, 0) - offset
    c = lax.broadcasted_iota(jnp.int32, shape, 1)
    inside = (r >= 0) & (r < FOLD)
    return ((r - c + 2 * COLS) % MODES == 0).astype(F32) * inside.astype(F32)


def shared(left, right):
    size = left.shape[0]
    shape = (size, size + 1)
    r = lax.broadcasted_iota(jnp.int32, shape, 0)
    low = lax.broadcasted_iota(jnp.int32, shape, 1) <= r
    blank = jnp.zeros((size, 1), F32)
    return jnp.where(low, jnp.concatenate([right, blank], axis=1), jnp.concatenate([blank, left], axis=1))


def unshared(both):
    size = both.shape[0]
    left, right = both[:, 1 : size + 1], both[:, 0:size]
    keep = upper(size)
    return jnp.where(keep, left, left.T), jnp.where(keep, right.T, right)


def unpacked(pay):
    t = THIRD
    first, second = unshared(pay[0:COLS, 0 : COLS + 1])
    at = COLS + 1
    r = lax.broadcasted_iota(jnp.int32, (COLS, COLS), 0)
    c = lax.broadcasted_iota(jnp.int32, (COLS, COLS), 1)
    zeroth = mm(pay[0:COLS, at : at + MODES], chosen((MODES, COLS), 0))
    zeroth = jnp.where(((r * 43) >> 8) == ((c * 43) >> 8), zeroth, 0.0)
    at, half = at + MODES, t // 2 + 1
    middle, end = unshared(
        jnp.concatenate([pay[0:t, at : at + half], pay[t : 2 * t, at : at + half - 1]], axis=1)
    )
    block = [pay[COLS : COLS + t, t * k : t * (k + 1)] for k in range(4)]
    third = jnp.concatenate(
        [
            jnp.concatenate([block[3], block[0], block[1]], axis=1),
            jnp.concatenate([block[0].T, middle, block[2]], axis=1),
            jnp.concatenate([block[1].T, block[2].T, end], axis=1),
        ],
        axis=0,
    )
    return zeroth, first, second, third


class Rows:
    def __init__(self, nx, ny, nz, info, centers, base, fext, qext):
        self.nx, self.ny, self.nz, self.ey = nx, ny, nz, ny + 4
        self.info, self.centers = info, centers
        self.base, self.fext, self.qext = base, fext, qext
        row = lax.broadcasted_iota(jnp.int32, (FOLD, nz), 0)
        body = (row * 43) >> 8
        mode = row - MODES * body
        self.is_mode = [mode == m for m in range(MODES)]
        self.bodies = [(body + k * (FOLD // MODES)).astype(F32) for k in range(COLS // FOLD)]

    def describe(self, cells, layer, rows, first_y, shifts):
        nz, base, info = self.nz, self.base, self.info
        tags, index, fluid = cells
        lane = lax.broadcasted_iota(jnp.int32, tags.shape, 1)
        y = lax.broadcasted_iota(jnp.int32, tags.shape, 0) + (info[1] + first_y)
        shifted = index + (index >= 13).astype(jnp.int32)
        part_x = (shifted >= 9).astype(jnp.int32) + (shifted >= 18).astype(jnp.int32)
        rest = shifted - 9 * part_x
        part_y = (rest >= 3).astype(jnp.int32) + (rest >= 6).astype(jnp.int32)
        part_z = rest - 3 * part_y
        comps = [(part - 1).astype(F32) for part in (part_x, part_y, part_z)]
        inverse = 1.0 / jnp.sqrt(comps[0] * comps[0] + comps[1] * comps[1] + comps[2] * comps[2])
        fl = fluid.astype(F32)
        n_x, n_y, n_z = (comp * inverse * fl for comp in comps)
        place = [jnp.zeros(tags.shape, F32)] * 3
        for b in range(BODIES):
            here = tags == b
            place = [jnp.where(here, self.centers[d, b], place[d]) for d in range(3)]
        pos_x = ((info[0] + (layer - 2)).astype(F32) + 0.5) / info[2].astype(F32)
        pos_y = (y.astype(F32) + 0.5) / info[3].astype(F32)
        pos_z = (lane.astype(F32) + 0.5) * (1.0 / nz)
        l_x, l_y, l_z = (3.0 * (pos - center) for pos, center in zip((pos_x, pos_y, pos_z), place))
        values = [n_x, n_y, n_z, l_y * n_z - l_z * n_y, l_z * n_x - l_x * n_z, l_x * n_y - l_y * n_x]
        for m, value in enumerate(values + [tags.astype(F32)]):
            base[m, layer, rows] = value
            if shifts:
                after = pltpu.roll(value, nz - 1, 1)
                before = pltpu.roll(value, 1, 1)
                if m == MODES:
                    after = jnp.where(lane == nz - 1, -1.0, after)
                    before = jnp.where(lane == 0, -1.0, before)
                base[NEXT + m, layer, rows] = after
                base[PREVIOUS + m, layer, rows] = before
        base[MASK, layer, rows] = fl

    def at(self, j):
        return jnp.where(j < 0, j + self.ey, jnp.where(j >= self.ey, j - self.ey, j))

    def row(self, which, i, j, rows):
        return jnp.broadcast_to(self.base[which, i, pl.ds(j, 1), :], (rows, self.nz))

    def sample(self, first, i, j):
        value = self.row(first, i, j, FOLD)
        for m in range(1, MODES):
            value = jnp.where(self.is_mode[m], self.row(first + m, i, j, FOLD), value)
        tag = self.row(first + MODES, i, j, FOLD)
        return jnp.concatenate([jnp.where(tag == bodies, value, 0.0) for bodies in self.bodies], axis=0)

    def forcing(self, i, j):
        j = self.at(j)
        self.fext[i, j] = self.sample(0, i, j)

    def both(self, i, j):
        j = self.at(j)
        self.fext[i, j] = self.sample(0, i, j)
        self.qext[i, j] = self.sample(NEXT, i, j) + self.sample(PREVIOUS, i, j)

    def apply(self, src, i, j, field, along_z):
        beside = src[i + 1, j] + src[i - 1, j]
        beside = beside + src[i, self.at(j + 1)] + src[i, self.at(j - 1)]
        beside = beside + along_z
        return field + self.row(MASK, i, j, COLS) * (5.0 * field - beside)

    def operated(self, i, j):
        j = self.at(j)
        self.qext[i, j] = self.apply(self.fext, i, j, self.fext[i, j], self.qext[i, j])

    def collect(self, i, j, cells, lh, rh):
        nz = self.nz
        lane = lax.broadcasted_iota(jnp.int32, (COLS, nz), 1)
        forcing, field = self.fext[i, j], self.qext[i, j]
        up = jnp.where(lane >= 1, pltpu.roll(field, 1, 1), 0.0)
        down = jnp.where(lane < nz - 1, pltpu.roll(field, nz - 1, 1), 0.0)
        lh[0:COLS, cells] = forcing
        lh[COLS : 2 * COLS, cells] = field
        rh[0:COLS, cells] = field
        rh[COLS : 2 * COLS, cells] = self.apply(self.qext, i, j, field, up + down)
        fold = forcing[0:FOLD]
        for k in range(1, COLS // FOLD):
            fold = fold + forcing[k * FOLD : (k + 1) * FOLD]
        rh[2 * COLS : 2 * COLS + FOLD, cells] = fold


    @staticmethod
    def pack(grams, pay):
        first, second = grams[0:COLS, 0:COLS], grams[COLS : 2 * COLS, 0:COLS]
        third = grams[COLS : 2 * COLS, COLS : 2 * COLS]
        t = THIRD
        zeroth = mm(grams[0:COLS, 2 * COLS : 2 * COLS + FOLD], chosen((FOLD, MODES), 0))
        blocks = [[third[t * p : t * (p + 1), t * q : t * (q + 1)] for q in range(3)] for p in range(3)]
        ends = shared(blocks[1][1], blocks[2][2])
        half = t // 2 + 1
        ends = jnp.concatenate([ends[:, :half], jnp.pad(ends[:, half:], ((0, t), (0, 1)))], axis=0)
        unused = jnp.zeros((COLS, 128 - COLS - 1 - MODES - half), F32)
        pay[0:COLS, :] = jnp.concatenate([shared(first, second), zeroth, ends, unused], axis=1)
        pay[COLS : COLS + t, :] = jnp.concatenate([blocks[0][1], blocks[0][2], blocks[1][2], blocks[0][0]], axis=1)


def own_kernel(nx, ny, nz, info, centers, own, kept_in, base, fext, qext, kept):
    kept[...] = kept_in[...]
    rows = Rows(nx, ny, nz, info, centers, base, fext, qext)
    for layer in range(nx):
        rows.describe([own[k, layer] for k in range(3)], layer + 2, pl.ds(0, ny), 0, True)
    for i in range(2, nx + 2):

        @pl.loop(0, ny, unroll=True)
        def _(j, i=i):
            rows.both(i, j)


def inner_kernel(nx, ny, nz, info, centers, across, pair, base_in, fext_in, qext_in, base, fext, qext, lh, gram, rh):
    del base_in, fext_in, qext_in
    rows = Rows(nx, ny, nz, info, centers, base, fext, qext)
    core = info[4]
    other, beyond = pair[...], across[...]
    before = jnp.where(core == 0, beyond, other)
    after = jnp.where(core == 0, other, beyond)
    for layer in range(nx):
        rows.describe([before[k, layer] for k in range(3)], layer, pl.ds(0, ny), 0, layer == nx - 1)
        rows.describe([after[k, layer] for k in range(3)], layer + 2 + nx, pl.ds(0, ny), 0, layer == 0)
    for i in (0, 1, nx + 2, nx + 3):

        @pl.loop(0, ny, unroll=True)
        def _(j, i=i):
            if i in (1, nx + 2):
                rows.both(i, j)
            else:
                rows.forcing(i, j)

    for i in range(1, nx + 3):

        @pl.loop(1, ny - 1, unroll=True)
        def _(j, i=i):
            rows.operated(i, j)

    for i in range(2, nx + 2):

        @pl.loop(0, ny - 4, unroll=True)
        def _(k, i=i):
            cells = pl.ds(pl.multiple_of(((i - 2) * (ny - 4) + k) * nz, nz), nz)
            rows.collect(i, k + 2, cells, lh, rh)

    gram[...] = dot(lh[...], rh[...], ((1,), (1,)))


def outer_kernel(
    nx, ny, nz, info, centers, odd, even, base_in, fext_in, qext_in, gram, base, fext, qext, lh, pay, rh
):
    del base_in, fext_in, qext_in
    rows = Rows(nx, ny, nz, info, centers, base, fext, qext)
    parity = info[5]
    above = jnp.where(parity == 0, even[...], odd[...])
    below = jnp.where(parity == 0, odd[...], even[...])
    for layer in range(nx + 2):
        rows.describe([above[k, layer] for k in range(3)], layer + 1, pl.ds(ny, 2), ny, True)
        rows.describe([below[k, layer] for k in range(3)], layer + 1, pl.ds(ny + 2, 2), -2, True)
    for i in range(1, nx + 3):
        reach = 2 if 2 <= i < nx + 2 else 1
        for j in list(range(-reach, 0)) + list(range(ny, ny + reach)):
            if j in (-1, ny) and 2 <= i < nx + 2:
                rows.both(i, j)
            else:
                rows.forcing(i, j)
    for i in range(1, nx + 3):
        inside = 2 <= i < nx + 2

        @pl.loop(0, 2, unroll=True)
        def _(k, i=i):
            rows.operated(i, k * (ny - 1))

        if inside:

            @pl.loop(0, 2, unroll=True)
            def _(k, i=i):
                rows.operated(i, k * (ny + 1) - 1)

    for i in range(2, nx + 2):

        @pl.loop(0, 4, unroll=True)
        def _(k, i=i):
            cells = pl.ds(pl.multiple_of(((i - 2) * 4 + k) * nz, nz), nz)
            rows.collect(i, jnp.where(k < 2, k, k + ny - 4), cells, lh, rh)

    rows.pack(gram[...] + dot(lh[...], rh[...], ((1,), (1,))), pay)


def inverse_spd(matrix, work):
    size = matrix.shape[0]
    r = lax.broadcasted_iota(jnp.int32, (size, size), 0)
    c = lax.broadcasted_iota(jnp.int32, (size, size), 1)
    diagonal = jnp.where(r == c, matrix, 0.0)
    scale_r = lax.rsqrt(jnp.sum(diagonal, axis=1, keepdims=True))
    scale_c = lax.rsqrt(jnp.sum(diagonal, axis=0, keepdims=True))
    scaled = matrix * scale_r * scale_c
    square = mm(scaled, scaled)
    bound = jnp.max(jnp.sum(jnp.abs(square), axis=0, keepdims=True), axis=1, keepdims=True)
    weight = lax.rsqrt(bound)
    eye = (r == c).astype(F32)
    work[0:size] = (30.0 / 7.0) * eye - (25.0 / 7.0 * weight) * scaled
    work[size : 2 * size] = eye - (30.0 / 7.0 * weight) * scaled + (25.0 / 7.0 * weight * weight) * square

    def longer(carry):
        power = work[size : 2 * size]
        more = mm(work[...], power)
        work[0:size] = work[0:size] + more[:size]
        work[size : 2 * size] = more[size:]
        return carry[0] + 1, jnp.sum(power * power) > 2e-6

    lax.while_loop(lambda carry: (carry[0] < 28) & carry[1], longer, (jnp.int32(0), jnp.bool_(True)))
    return work[0:size] * (weight * scale_r) * scale_c


def solve_kernel(nx, ny, nz, scale, pay, inner, outer, out, added, work):
    zeroth, first, second, third = unpacked(pay)
    center = jnp.where(on_diagonal(COLS), second / first, 0.0)
    shift = jnp.sum(jnp.sum(center, axis=1, keepdims=True), axis=0, keepdims=True) * (1.0 / COLS)
    cross = second - shift * first
    energy = jnp.concatenate(
        [
            jnp.concatenate([first, cross], axis=1),
            jnp.concatenate([cross, third - shift * (second + cross)], axis=1),
        ],
        axis=0,
    )
    solved = mm(inverse_spd(energy, work), jnp.concatenate([zeroth, first - shift * zeroth], axis=0))
    later = solved[COLS:]
    early = solved[:COLS] - shift * later
    coeffs = jnp.concatenate([early, later], axis=0)
    rows = nx * ny
    for lh, places in ((inner, range(2, ny - 2)), (outer, [0, 1, ny - 2, ny - 1])):
        values = dot(coeffs, lh[...], ((0,), (0,)))
        for k, (i, j) in enumerate((i, j) for i in range(nx) for j in places):
            out[pl.ds(i * ny + j, COLS, stride=rows), :] = values[:, k * nz : (k + 1) * nz]
    added[...] = (mm(zeroth, early) + mm(first, later)) * scale


def swap(array, axes, start):
    size = lax.axis_size(axes)
    pairs = [(i, i + 1) for i in range(start, size - 1, 2)]
    return lax.ppermute(array, axes, pairs + [(j, i) for i, j in pairs])


def reduced(part):
    near, far = (lax.axis_size(axes) for axes in (NEAR, FAR))
    rows, lanes = part.shape
    piece = lax.all_to_all(part, NEAR, 0, 0, tiled=True).reshape(near, rows // near, lanes).sum(0)
    piece = lax.all_to_all(jnp.broadcast_to(piece[None], (far,) + piece.shape), FAR, 0, 0, tiled=True).sum(0)
    return lax.all_to_all(
        jnp.broadcast_to(piece[None], (near,) + piece.shape), NEAR, 0, 0, tiled=True
    ).reshape(rows, lanes)


def shards(surface_tags, normal_index, fluid_mask, body_centers):
    nx, ny, nz = surface_tags.shape
    count_x = nx * lax.axis_size(GX)
    count_y = ny * lax.axis_size(GY)
    at_x, at_y, core = lax.axis_index(GX), lax.axis_index(GY), lax.axis_index("c")
    own = lax.optimization_barrier(jnp.stack([surface_tags, normal_index, fluid_mask]))
    across = swap(own, GX, 1)
    pair = lax.ppermute(own, "c", [(0, 1), (1, 0)])
    before = jnp.where(core == 1, pair, across)[:, nx - 1 :]
    after = jnp.where(core == 0, pair, across)[:, :1]
    near = jnp.concatenate([before, own, after], axis=1)
    first, last = near[:, :, :2], near[:, :, ny - 2 :]
    parity = at_y % 2
    even = swap(jnp.where(parity == 0, last, first), GY, 0)
    odd = swap(jnp.where(parity == 0, first, last), GY, 1)
    info = jnp.stack(
        [at_x * nx, at_y * ny, jnp.int32(count_x), jnp.int32(count_y), core, parity]
    ).astype(jnp.int32)
    half = nx * ny * nz // 2
    centers = body_centers.T
    ex, ey = nx + 4, ny + 4
    vmem = pl.BlockSpec(memory_space=pltpu.VMEM)
    smem = pl.BlockSpec(memory_space=pltpu.SMEM)

    def shape(*dims):
        return jax.ShapeDtypeStruct(dims, F32)

    def call(kernel, outs, ins, scratch, flops, aliases, name):
        return pl.pallas_call(
            functools.partial(kernel, nx, ny, nz),
            out_shape=outs,
            in_specs=[smem, smem] + [vmem] * (len(ins) - 2),
            out_specs=tuple(vmem for _ in outs),
            scratch_shapes=scratch,
            input_output_aliases=aliases,
            compiler_params=pltpu.CompilerParams(vmem_limit_bytes=24 * 1024 * 1024),
            cost_estimate=pl.CostEstimate(flops=flops, bytes_accessed=8 * 1024 * 1024, transcendentals=0),
            name=name,
        )(*ins)

    base, field = shape(MASK + 1, ex, ey, nz), shape(ex, ey, COLS, nz)
    base, fext, qext, kept = call(
        own_kernel, (base, field, field, shape(3, BODIES)),
        (info, centers, own, centers), [], 1 << 28, {}, "own_rows",
    )
    rh = [pltpu.VMEM((2 * COLS + FOLD, half), F32)]
    base, fext, qext, inner, gram = call(
        inner_kernel,
        (shape(*base.shape), shape(*fext.shape), shape(*qext.shape), shape(2 * COLS, half), shape(2 * COLS, 2 * COLS + FOLD)),
        (info, kept, across, pair, base, fext, qext), rh, 1 << 29, {4: 0, 5: 1, 6: 2}, "inner_rows",
    )
    _, _, _, outer, pay = call(
        outer_kernel,
        (shape(*base.shape), shape(*fext.shape), shape(*qext.shape), shape(2 * COLS, half), shape(COLS + THIRD, 128)),
        (info, kept, odd, even, base, fext, qext, gram), rh, 1 << 29, {4: 0, 5: 1, 6: 2}, "outer_rows",
    )
    pay = reduced(pay)
    scale = 8.0 * BODIES / (count_x * count_y * nz)
    pressure, added = pl.pallas_call(
        functools.partial(solve_kernel, nx, ny, nz, scale),
        out_shape=(
            jax.ShapeDtypeStruct((COLS * nx * ny, nz), F32),
            jax.ShapeDtypeStruct((COLS, COLS), F32),
        ),
        in_specs=[vmem] * 3,
        out_specs=(vmem, vmem),
        scratch_shapes=[pltpu.VMEM((4 * COLS, 2 * COLS), F32)],
        compiler_params=pltpu.CompilerParams(vmem_limit_bytes=24 * 1024 * 1024),
        name="solve",
    )(pay, inner, outer)
    return pressure.reshape(COLS, nx, ny, nz), added


def solution(mesh):
    split = Mesh(np.asarray(mesh.devices).reshape(4, 4, 2, 4, 4), GX + GY)
    return jax.shard_map(
        shards,
        mesh=split,
        in_specs=(P(GX, GY, None), P(GX, GY, None), P(GX, GY, None), P()),
        out_specs=(P(None, GX, GY, None), P()),
        check_vma=False,
    )
```

```python
import functools

import jax
import jax.numpy as jnp
import numpy as np
from jax import lax
from jax.experimental import pallas as pl
from jax.experimental.pallas import tpu as pltpu
from jax.sharding import Mesh, PartitionSpec as P

BODIES = 16
MODES = 6
COLS = BODIES * MODES
FOLD = 4 * MODES
GX = ("y", "zh", "c")
GY = ("x", "zl")
NEAR = ("y", "c", "x")
FAR = ("zh", "zl")
F32 = jnp.float32


def dot(left, right, dims):
    return lax.dot_general(
        left, right, (dims, ((), ())), precision=lax.Precision.HIGHEST, preferred_element_type=F32
    )


def mm(left, right):
    return dot(left, right, ((1,), (0,)))


THIRD = COLS // 3
NEXT = MODES + 1
PREVIOUS = 2 * NEXT
MASK = 3 * NEXT


def upper(size):
    r = lax.broadcasted_iota(jnp.int32, (size, size), 0)
    return r <= lax.broadcasted_iota(jnp.int32, (size, size), 1)


def on_diagonal(size):
    r = lax.broadcasted_iota(jnp.int32, (size, size), 0)
    return r == lax.broadcasted_iota(jnp.int32, (size, size), 1)


def chosen(shape, offset):
    r = lax.broadcasted_iota(jnp.int32, shape, 0) - offset
    c = lax.broadcasted_iota(jnp.int32, shape, 1)
    inside = (r >= 0) & (r < FOLD)
    return ((r - c + 2 * COLS) % MODES == 0).astype(F32) * inside.astype(F32)


def shared(left, right):
    size = left.shape[0]
    shape = (size, size + 1)
    r = lax.broadcasted_iota(jnp.int32, shape, 0)
    low = lax.broadcasted_iota(jnp.int32, shape, 1) <= r
    blank = jnp.zeros((size, 1), F32)
    return jnp.where(low, jnp.concatenate([right, blank], axis=1), jnp.concatenate([blank, left], axis=1))


def unshared(both):
    size = both.shape[0]
    left, right = both[:, 1 : size + 1], both[:, 0:size]
    keep = upper(size)
    return jnp.where(keep, left, left.T), jnp.where(keep, right.T, right)


def unpacked(pay):
    t = THIRD
    first, second = unshared(pay[0:COLS, 0 : COLS + 1])
    at = COLS + 1
    r = lax.broadcasted_iota(jnp.int32, (COLS, COLS), 0)
    c = lax.broadcasted_iota(jnp.int32, (COLS, COLS), 1)
    zeroth = mm(pay[0:COLS, at : at + MODES], chosen((MODES, COLS), 0))
    zeroth = jnp.where(((r * 43) >> 8) == ((c * 43) >> 8), zeroth, 0.0)
    at, half = at + MODES, t // 2 + 1
    middle, end = unshared(
        jnp.concatenate([pay[0:t, at : at + half], pay[t : 2 * t, at : at + half - 1]], axis=1)
    )
    block = [pay[COLS : COLS + t, t * k : t * (k + 1)] for k in range(4)]
    third = jnp.concatenate(
        [
            jnp.concatenate([block[3], block[0], block[1]], axis=1),
            jnp.concatenate([block[0].T, middle, block[2]], axis=1),
            jnp.concatenate([block[1].T, block[2].T, end], axis=1),
        ],
        axis=0,
    )
    return zeroth, first, second, third


class Rows:
    def __init__(self, nx, ny, nz, info, centers, base, fext, qext):
        self.nx, self.ny, self.nz, self.ey = nx, ny, nz, ny + 4
        self.info, self.centers = info, centers
        self.base, self.fext, self.qext = base, fext, qext
        row = lax.broadcasted_iota(jnp.int32, (FOLD, nz), 0)
        body = (row * 43) >> 8
        mode = row - MODES * body
        self.is_mode = [mode == m for m in range(MODES)]
        self.bodies = [(body + k * (FOLD // MODES)).astype(F32) for k in range(COLS // FOLD)]

    def describe(self, cells, layer, rows, first_y, shifts):
        nz, base, info = self.nz, self.base, self.info
        tags, index, fluid = cells
        lane = lax.broadcasted_iota(jnp.int32, tags.shape, 1)
        y = lax.broadcasted_iota(jnp.int32, tags.shape, 0) + (info[1] + first_y)
        shifted = index + (index >= 13).astype(jnp.int32)
        part_x = (shifted >= 9).astype(jnp.int32) + (shifted >= 18).astype(jnp.int32)
        rest = shifted - 9 * part_x
        part_y = (rest >= 3).astype(jnp.int32) + (rest >= 6).astype(jnp.int32)
        part_z = rest - 3 * part_y
        comps = [(part - 1).astype(F32) for part in (part_x, part_y, part_z)]
        inverse = 1.0 / jnp.sqrt(comps[0] * comps[0] + comps[1] * comps[1] + comps[2] * comps[2])
        fl = fluid.astype(F32)
        n_x, n_y, n_z = (comp * inverse * fl for comp in comps)
        place = [jnp.zeros(tags.shape, F32)] * 3
        for b in range(BODIES):
            here = tags == b
            place = [jnp.where(here, self.centers[d, b], place[d]) for d in range(3)]
        pos_x = ((info[0] + (layer - 2)).astype(F32) + 0.5) / info[2].astype(F32)
        pos_y = (y.astype(F32) + 0.5) / info[3].astype(F32)
        pos_z = (lane.astype(F32) + 0.5) * (1.0 / nz)
        l_x, l_y, l_z = (3.0 * (pos - center) for pos, center in zip((pos_x, pos_y, pos_z), place))
        values = [n_x, n_y, n_z, l_y * n_z - l_z * n_y, l_z * n_x - l_x * n_z, l_x * n_y - l_y * n_x]
        for m, value in enumerate(values + [tags.astype(F32)]):
            base[m, layer, rows] = value
            if shifts:
                after = pltpu.roll(value, nz - 1, 1)
                before = pltpu.roll(value, 1, 1)
                if m == MODES:
                    after = jnp.where(lane == nz - 1, -1.0, after)
                    before = jnp.where(lane == 0, -1.0, before)
                base[NEXT + m, layer, rows] = after
                base[PREVIOUS + m, layer, rows] = before
        base[MASK, layer, rows] = fl

    def at(self, j):
        return jnp.where(j < 0, j + self.ey, jnp.where(j >= self.ey, j - self.ey, j))

    def row(self, which, i, j, rows):
        return jnp.broadcast_to(self.base[which, i, pl.ds(j, 1), :], (rows, self.nz))

    def sample(self, first, i, j):
        value = self.row(first, i, j, FOLD)
        for m in range(1, MODES):
            value = jnp.where(self.is_mode[m], self.row(first + m, i, j, FOLD), value)
        tag = self.row(first + MODES, i, j, FOLD)
        return jnp.concatenate([jnp.where(tag == bodies, value, 0.0) for bodies in self.bodies], axis=0)

    def forcing(self, i, j):
        j = self.at(j)
        self.fext[i, j] = self.sample(0, i, j)

    def both(self, i, j):
        j = self.at(j)
        self.fext[i, j] = self.sample(0, i, j)
        self.qext[i, j] = self.sample(NEXT, i, j) + self.sample(PREVIOUS, i, j)

    def apply(self, src, i, j, field, along_z):
        beside = src[i + 1, j] + src[i - 1, j]
        beside = beside + src[i, self.at(j + 1)] + src[i, self.at(j - 1)]
        beside = beside + along_z
        return field + self.row(MASK, i, j, COLS) * (5.0 * field - beside)

    def operated(self, i, j):
        j = self.at(j)
        self.qext[i, j] = self.apply(self.fext, i, j, self.fext[i, j], self.qext[i, j])

    def collect(self, i, j, cells, lh, rh):
        nz = self.nz
        lane = lax.broadcasted_iota(jnp.int32, (COLS, nz), 1)
        forcing, field = self.fext[i, j], self.qext[i, j]
        up = jnp.where(lane >= 1, pltpu.roll(field, 1, 1), 0.0)
        down = jnp.where(lane < nz - 1, pltpu.roll(field, nz - 1, 1), 0.0)
        lh[0:COLS, cells] = forcing
        lh[COLS : 2 * COLS, cells] = field
        rh[0:COLS, cells] = field
        rh[COLS : 2 * COLS, cells] = self.apply(self.qext, i, j, field, up + down)
        fold = forcing[0:FOLD]
        for k in range(1, COLS // FOLD):
            fold = fold + forcing[k * FOLD : (k + 1) * FOLD]
        rh[2 * COLS : 2 * COLS + FOLD, cells] = fold


    @staticmethod
    def pack(grams, pay):
        first, second = grams[0:COLS, 0:COLS], grams[COLS : 2 * COLS, 0:COLS]
        third = grams[COLS : 2 * COLS, COLS : 2 * COLS]
        t = THIRD
        zeroth = mm(grams[0:COLS, 2 * COLS : 2 * COLS + FOLD], chosen((FOLD, MODES), 0))
        blocks = [[third[t * p : t * (p + 1), t * q : t * (q + 1)] for q in range(3)] for p in range(3)]
        ends = shared(blocks[1][1], blocks[2][2])
        half = t // 2 + 1
        ends = jnp.concatenate([ends[:, :half], jnp.pad(ends[:, half:], ((0, t), (0, 1)))], axis=0)
        unused = jnp.zeros((COLS, 128 - COLS - 1 - MODES - half), F32)
        pay[0:COLS, :] = jnp.concatenate([shared(first, second), zeroth, ends, unused], axis=1)
        pay[COLS : COLS + t, :] = jnp.concatenate([blocks[0][1], blocks[0][2], blocks[1][2], blocks[0][0]], axis=1)


def own_kernel(nx, ny, nz, info, centers, own, kept_in, base, fext, qext, kept):
    kept[...] = kept_in[...]
    rows = Rows(nx, ny, nz, info, centers, base, fext, qext)
    for layer in range(nx):
        rows.describe([own[k, layer] for k in range(3)], layer + 2, pl.ds(0, ny), 0, True)
    for i in range(2, nx + 2):

        @pl.loop(0, ny, unroll=True)
        def _(j, i=i):
            rows.both(i, j)


def inner_kernel(nx, ny, nz, info, centers, across, pair, base_in, fext_in, qext_in, base, fext, qext, lh, gram, rh):
    del base_in, fext_in, qext_in
    rows = Rows(nx, ny, nz, info, centers, base, fext, qext)
    core = info[4]
    other, beyond = pair[...], across[...]
    before = jnp.where(core == 0, beyond, other)
    after = jnp.where(core == 0, other, beyond)
    for layer in range(nx):
        rows.describe([before[k, layer] for k in range(3)], layer, pl.ds(0, ny), 0, layer == nx - 1)
        rows.describe([after[k, layer] for k in range(3)], layer + 2 + nx, pl.ds(0, ny), 0, layer == 0)
    for i in (0, 1, nx + 2, nx + 3):

        @pl.loop(0, ny, unroll=True)
        def _(j, i=i):
            if i in (1, nx + 2):
                rows.both(i, j)
            else:
                rows.forcing(i, j)

    for i in range(1, nx + 3):

        @pl.loop(1, ny - 1, unroll=True)
        def _(j, i=i):
            rows.operated(i, j)

    for i in range(2, nx + 2):

        @pl.loop(0, ny - 4, unroll=True)
        def _(k, i=i):
            cells = pl.ds(pl.multiple_of(((i - 2) * (ny - 4) + k) * nz, nz), nz)
            rows.collect(i, k + 2, cells, lh, rh)

    gram[...] = dot(lh[...], rh[...], ((1,), (1,)))


def outer_kernel(
    nx, ny, nz, info, centers, odd, even, base_in, fext_in, qext_in, gram, base, fext, qext, lh, pay, rh
):
    del base_in, fext_in, qext_in
    rows = Rows(nx, ny, nz, info, centers, base, fext, qext)
    parity = info[5]
    above = jnp.where(parity == 0, even[...], odd[...])
    below = jnp.where(parity == 0, odd[...], even[...])
    for layer in range(nx + 2):
        rows.describe([above[k, layer] for k in range(3)], layer + 1, pl.ds(ny, 2), ny, True)
        rows.describe([below[k, layer] for k in range(3)], layer + 1, pl.ds(ny + 2, 2), -2, True)
    for i in range(1, nx + 3):
        reach = 2 if 2 <= i < nx + 2 else 1
        for j in list(range(-reach, 0)) + list(range(ny, ny + reach)):
            if j in (-1, ny) and 2 <= i < nx + 2:
                rows.both(i, j)
            else:
                rows.forcing(i, j)
    for i in range(1, nx + 3):
        inside = 2 <= i < nx + 2

        @pl.loop(0, 2, unroll=True)
        def _(k, i=i):
            rows.operated(i, k * (ny - 1))

        if inside:

            @pl.loop(0, 2, unroll=True)
            def _(k, i=i):
                rows.operated(i, k * (ny + 1) - 1)

    for i in range(2, nx + 2):

        @pl.loop(0, 4, unroll=True)
        def _(k, i=i):
            cells = pl.ds(pl.multiple_of(((i - 2) * 4 + k) * nz, nz), nz)
            rows.collect(i, jnp.where(k < 2, k, k + ny - 4), cells, lh, rh)

    rows.pack(gram[...] + dot(lh[...], rh[...], ((1,), (1,))), pay)


def solve_spd(turned, matrix, work):
    size = matrix.shape[0]
    r = lax.broadcasted_iota(jnp.int32, (size, size), 0)
    c = lax.broadcasted_iota(jnp.int32, (size, size), 1)
    diagonal = jnp.where(r == c, matrix, 0.0)
    scale_r = lax.rsqrt(jnp.sum(diagonal, axis=1, keepdims=True))
    scale_c = lax.rsqrt(jnp.sum(diagonal, axis=0, keepdims=True))
    scaled = matrix * scale_r * scale_c
    turned = turned * scale_c
    work[0:size] = scaled
    work[size:] = turned
    product = mm(work[...], scaled)
    square = product[:size]
    bound = jnp.max(jnp.sum(jnp.abs(square), axis=0, keepdims=True), axis=1, keepdims=True)
    weight = lax.rsqrt(bound)
    eye = (r == c).astype(F32)
    work[0:size] = eye - (30.0 / 7.0 * weight) * scaled + (25.0 / 7.0 * weight * weight) * square
    work[size:] = (30.0 / 7.0) * turned - (25.0 / 7.0 * weight) * product[size:]

    def longer(carry):
        power = work[0:size]
        more = mm(work[...], power)
        work[0:size] = more[:size]
        work[size:] = work[size:] + more[size:]
        return carry[0] + 1, jnp.sum(power * power) > 2e-6

    lax.while_loop(lambda carry: (carry[0] < 28) & carry[1], longer, (jnp.int32(0), jnp.bool_(True)))
    return work[size:] * (weight * scale_c)


def solve_kernel(nx, ny, nz, scale, pay, inner, outer, out, added, work):
    zeroth, first, second, third = unpacked(pay)
    center = jnp.where(on_diagonal(COLS), second / first, 0.0)
    shift = jnp.sum(jnp.sum(center, axis=1, keepdims=True), axis=0, keepdims=True) * (1.0 / COLS)
    cross = second - shift * first
    energy = jnp.concatenate(
        [
            jnp.concatenate([first, cross], axis=1),
            jnp.concatenate([cross, third - shift * (second + cross)], axis=1),
        ],
        axis=0,
    )
    solved = solve_spd(jnp.concatenate([zeroth, first - shift * zeroth], axis=1), energy, work)
    later = solved[:, COLS:]
    early = solved[:, :COLS] - shift * later
    coeffs = jnp.concatenate([early, later], axis=1)
    rows = nx * ny
    for lh, places in ((inner, range(2, ny - 2)), (outer, [0, 1, ny - 2, ny - 1])):
        values = mm(coeffs, lh[...])
        for k, (i, j) in enumerate((i, j) for i in range(nx) for j in places):
            out[pl.ds(i * ny + j, COLS, stride=rows), :] = values[:, k * nz : (k + 1) * nz]
    added[...] = (mm(early, zeroth) + mm(later, first)).T * scale


def swap(array, axes, start):
    size = lax.axis_size(axes)
    pairs = [(i, i + 1) for i in range(start, size - 1, 2)]
    return lax.ppermute(array, axes, pairs + [(j, i) for i, j in pairs])


def reduced(part):
    near, far = (lax.axis_size(axes) for axes in (NEAR, FAR))
    rows, lanes = part.shape
    piece = lax.all_to_all(part, NEAR, 0, 0, tiled=True).reshape(near, rows // near, lanes).sum(0)
    piece = lax.all_to_all(jnp.broadcast_to(piece[None], (far,) + piece.shape), FAR, 0, 0, tiled=True).sum(0)
    return lax.all_to_all(
        jnp.broadcast_to(piece[None], (near,) + piece.shape), NEAR, 0, 0, tiled=True
    ).reshape(rows, lanes)


def shards(surface_tags, normal_index, fluid_mask, body_centers):
    nx, ny, nz = surface_tags.shape
    count_x = nx * lax.axis_size(GX)
    count_y = ny * lax.axis_size(GY)
    at_x, at_y, core = lax.axis_index(GX), lax.axis_index(GY), lax.axis_index("c")
    own = lax.optimization_barrier(jnp.stack([surface_tags, normal_index, fluid_mask]))
    across = swap(own, GX, 1)
    pair = lax.ppermute(own, "c", [(0, 1), (1, 0)])
    before = jnp.where(core == 1, pair, across)[:, nx - 1 :]
    after = jnp.where(core == 0, pair, across)[:, :1]
    near = jnp.concatenate([before, own, after], axis=1)
    first, last = near[:, :, :2], near[:, :, ny - 2 :]
    parity = at_y % 2
    even = swap(jnp.where(parity == 0, last, first), GY, 0)
    odd = swap(jnp.where(parity == 0, first, last), GY, 1)
    info = jnp.stack(
        [at_x * nx, at_y * ny, jnp.int32(count_x), jnp.int32(count_y), core, parity]
    ).astype(jnp.int32)
    half = nx * ny * nz // 2
    centers = body_centers.T
    ex, ey = nx + 4, ny + 4
    vmem = pl.BlockSpec(memory_space=pltpu.VMEM)
    smem = pl.BlockSpec(memory_space=pltpu.SMEM)

    def shape(*dims):
        return jax.ShapeDtypeStruct(dims, F32)

    def call(kernel, outs, ins, scratch, flops, aliases, name):
        return pl.pallas_call(
            functools.partial(kernel, nx, ny, nz),
            out_shape=outs,
            in_specs=[smem, smem] + [vmem] * (len(ins) - 2),
            out_specs=tuple(vmem for _ in outs),
            scratch_shapes=scratch,
            input_output_aliases=aliases,
            compiler_params=pltpu.CompilerParams(vmem_limit_bytes=24 * 1024 * 1024),
            cost_estimate=pl.CostEstimate(flops=flops, bytes_accessed=8 * 1024 * 1024, transcendentals=0),
            name=name,
        )(*ins)

    base, field = shape(MASK + 1, ex, ey, nz), shape(ex, ey, COLS, nz)
    base, fext, qext, kept = call(
        own_kernel, (base, field, field, shape(3, BODIES)),
        (info, centers, own, centers), [], 1 << 28, {}, "own_rows",
    )
    rh = [pltpu.VMEM((2 * COLS + FOLD, half), F32)]
    base, fext, qext, inner, gram = call(
        inner_kernel,
        (shape(*base.shape), shape(*fext.shape), shape(*qext.shape), shape(2 * COLS, half), shape(2 * COLS, 2 * COLS + FOLD)),
        (info, kept, across, pair, base, fext, qext), rh, 1 << 29, {4: 0, 5: 1, 6: 2}, "inner_rows",
    )
    _, _, _, outer, pay = call(
        outer_kernel,
        (shape(*base.shape), shape(*fext.shape), shape(*qext.shape), shape(2 * COLS, half), shape(COLS + THIRD, 128)),
        (info, kept, odd, even, base, fext, qext, gram), rh, 1 << 29, {4: 0, 5: 1, 6: 2}, "outer_rows",
    )
    pay = reduced(pay)
    scale = 8.0 * BODIES / (count_x * count_y * nz)
    pressure, added = pl.pallas_call(
        functools.partial(solve_kernel, nx, ny, nz, scale),
        out_shape=(
            jax.ShapeDtypeStruct((COLS * nx * ny, nz), F32),
            jax.ShapeDtypeStruct((COLS, COLS), F32),
        ),
        in_specs=[vmem] * 3,
        out_specs=(vmem, vmem),
        scratch_shapes=[pltpu.VMEM((3 * COLS, 2 * COLS), F32)],
        compiler_params=pltpu.CompilerParams(vmem_limit_bytes=24 * 1024 * 1024),
        name="solve",
    )(pay, inner, outer)
    return pressure.reshape(COLS, nx, ny, nz), added


def solution(mesh):
    split = Mesh(np.asarray(mesh.devices).reshape(4, 4, 2, 4, 4), GX + GY)
    return jax.shard_map(
        shards,
        mesh=split,
        in_specs=(P(GX, GY, None), P(GX, GY, None), P(GX, GY, None), P()),
        out_specs=(P(None, GX, GY, None), P()),
        check_vma=False,
    )
```

```python
import functools

import jax
import jax.numpy as jnp
import numpy as np
from jax import lax
from jax.experimental import pallas as pl
from jax.experimental.pallas import tpu as pltpu
from jax.sharding import Mesh, PartitionSpec as P

BODIES = 16
MODES = 6
COLS = BODIES * MODES
FOLD = 4 * MODES
GX = ("y", "zh", "c")
GY = ("x", "zl")
NEAR = ("c", "x", "y")
FAR = ("zh", "zl")
F32 = jnp.float32


def dot(left, right, dims):
    return lax.dot_general(
        left, right, (dims, ((), ())), precision=lax.Precision.HIGHEST, preferred_element_type=F32
    )


def mm(left, right):
    return dot(left, right, ((1,), (0,)))


THIRD = COLS // 3
NEXT = MODES + 1
PREVIOUS = 2 * NEXT
MASK = 3 * NEXT


def upper(size):
    r = lax.broadcasted_iota(jnp.int32, (size, size), 0)
    return r <= lax.broadcasted_iota(jnp.int32, (size, size), 1)


def on_diagonal(size):
    r = lax.broadcasted_iota(jnp.int32, (size, size), 0)
    return r == lax.broadcasted_iota(jnp.int32, (size, size), 1)


def same_mode(shape):
    r = lax.broadcasted_iota(jnp.int32, shape, 0)
    c = lax.broadcasted_iota(jnp.int32, shape, 1)
    return (c - MODES * ((c * 43) >> 8) == r).astype(F32)


def shared(left, right):
    size = left.shape[0]
    shape = (size, size + 1)
    r = lax.broadcasted_iota(jnp.int32, shape, 0)
    low = lax.broadcasted_iota(jnp.int32, shape, 1) <= r
    blank = jnp.zeros((size, 1), F32)
    return jnp.where(low, jnp.concatenate([right, blank], axis=1), jnp.concatenate([blank, left], axis=1))


def unshared(both):
    size = both.shape[0]
    left, right = both[:, 1 : size + 1], both[:, 0:size]
    keep = upper(size)
    return jnp.where(keep, left, left.T), jnp.where(keep, right.T, right)


def unpacked(pay):
    t = THIRD
    first, second = unshared(pay[0:COLS, 0 : COLS + 1])
    at = COLS + 1
    r = lax.broadcasted_iota(jnp.int32, (COLS, COLS), 0)
    c = lax.broadcasted_iota(jnp.int32, (COLS, COLS), 1)
    zeroth = mm(pay[0:COLS, at : at + MODES], same_mode((MODES, COLS)))
    zeroth = jnp.where(((r * 43) >> 8) == ((c * 43) >> 8), zeroth, 0.0)
    at, half = at + MODES, t // 2 + 1
    middle, end = unshared(
        jnp.concatenate([pay[0:t, at : at + half], pay[t : 2 * t, at : at + half - 1]], axis=1)
    )
    block = [pay[COLS : COLS + t, t * k : t * (k + 1)] for k in range(4)]
    third = jnp.concatenate(
        [
            jnp.concatenate([block[3], block[0], block[1]], axis=1),
            jnp.concatenate([block[0].T, middle, block[2]], axis=1),
            jnp.concatenate([block[1].T, block[2].T, end], axis=1),
        ],
        axis=0,
    )
    return zeroth, first, second, third


class Rows:
    def __init__(self, nx, ny, nz, info, centers, base, fext, qext):
        self.nx, self.ny, self.nz, self.ey = nx, ny, nz, ny + 4
        self.info, self.centers = info, centers
        self.base, self.fext, self.qext = base, fext, qext
        row = lax.broadcasted_iota(jnp.int32, (FOLD, nz), 0)
        body = (row * 43) >> 8
        mode = row - MODES * body
        self.is_mode = [mode == m for m in range(MODES)]
        self.bodies = [(body + k * (FOLD // MODES)).astype(F32) for k in range(COLS // FOLD)]

    def describe(self, cells, layer, rows, first_y, shifts):
        nz, base, info = self.nz, self.base, self.info
        tags, index, fluid = cells
        lane = lax.broadcasted_iota(jnp.int32, tags.shape, 1)
        y = lax.broadcasted_iota(jnp.int32, tags.shape, 0) + (info[1] + first_y)
        shifted = index + (index >= 13).astype(jnp.int32)
        part_x = (shifted >= 9).astype(jnp.int32) + (shifted >= 18).astype(jnp.int32)
        rest = shifted - 9 * part_x
        part_y = (rest >= 3).astype(jnp.int32) + (rest >= 6).astype(jnp.int32)
        part_z = rest - 3 * part_y
        comps = [(part - 1).astype(F32) for part in (part_x, part_y, part_z)]
        inverse = 1.0 / jnp.sqrt(comps[0] * comps[0] + comps[1] * comps[1] + comps[2] * comps[2])
        fl = fluid.astype(F32)
        active = jnp.where(tags < BODIES, fl, 0.0)
        n_x, n_y, n_z = (comp * inverse * active for comp in comps)
        place = [jnp.zeros(tags.shape, F32)] * 3
        for b in range(BODIES):
            here = tags == b
            place = [jnp.where(here, self.centers[d, b], place[d]) for d in range(3)]
        pos_x = ((info[0] + (layer - 2)).astype(F32) + 0.5) / info[2].astype(F32)
        pos_y = (y.astype(F32) + 0.5) / info[3].astype(F32)
        pos_z = (lane.astype(F32) + 0.5) * (1.0 / nz)
        l_x, l_y, l_z = (3.0 * (pos - center) for pos, center in zip((pos_x, pos_y, pos_z), place))
        values = [n_x, n_y, n_z, l_y * n_z - l_z * n_y, l_z * n_x - l_x * n_z, l_x * n_y - l_y * n_x]
        for m, value in enumerate(values + [tags.astype(F32)]):
            base[m, layer, rows] = value
            if shifts:
                after = pltpu.roll(value, nz - 1, 1)
                before = pltpu.roll(value, 1, 1)
                if m == MODES:
                    after = jnp.where(lane == nz - 1, -1.0, after)
                    before = jnp.where(lane == 0, -1.0, before)
                base[NEXT + m, layer, rows] = after
                base[PREVIOUS + m, layer, rows] = before
        base[MASK, layer, rows] = fl

    def at(self, j):
        return jnp.where(j < 0, j + self.ey, jnp.where(j >= self.ey, j - self.ey, j))

    def row(self, which, i, j, rows):
        return jnp.broadcast_to(self.base[which, i, pl.ds(j, 1), :], (rows, self.nz))

    def sample(self, first, i, j):
        value = self.row(first, i, j, FOLD)
        for m in range(1, MODES):
            value = jnp.where(self.is_mode[m], self.row(first + m, i, j, FOLD), value)
        tag = self.row(first + MODES, i, j, FOLD)
        return jnp.concatenate([jnp.where(tag == bodies, value, 0.0) for bodies in self.bodies], axis=0)

    def forcing(self, i, j):
        j = self.at(j)
        self.fext[i, j] = self.sample(0, i, j)

    def both(self, i, j):
        j = self.at(j)
        self.fext[i, j] = self.sample(0, i, j)
        self.qext[i, j] = self.sample(NEXT, i, j) + self.sample(PREVIOUS, i, j)

    def apply(self, src, i, j, field, along_z):
        beside = src[i + 1, j] + src[i - 1, j]
        beside = beside + src[i, self.at(j + 1)] + src[i, self.at(j - 1)]
        beside = beside + along_z
        return field + self.row(MASK, i, j, COLS) * (5.0 * field - beside)

    def operated(self, i, j):
        j = self.at(j)
        self.qext[i, j] = self.apply(self.fext, i, j, self.fext[i, j], self.qext[i, j])

    def collect(self, i, j, cells, lh, rh):
        nz = self.nz
        lane = lax.broadcasted_iota(jnp.int32, (COLS, nz), 1)
        forcing, field = self.fext[i, j], self.qext[i, j]
        up = jnp.where(lane >= 1, pltpu.roll(field, 1, 1), 0.0)
        down = jnp.where(lane < nz - 1, pltpu.roll(field, nz - 1, 1), 0.0)
        lh[0:COLS, cells] = forcing
        lh[COLS : 2 * COLS, cells] = field
        rh[0:COLS, cells] = field
        rh[COLS : 2 * COLS, cells] = self.apply(self.qext, i, j, field, up + down)
        for m in range(MODES):
            rh[2 * COLS + m : 2 * COLS + m + 1, cells] = self.base[m, i, pl.ds(j, 1), :]


    @staticmethod
    def pack(grams, pay):
        first, second = grams[0:COLS, 0:COLS], grams[COLS : 2 * COLS, 0:COLS]
        third = grams[COLS : 2 * COLS, COLS : 2 * COLS]
        t = THIRD
        zeroth = grams[0:COLS, 2 * COLS : 2 * COLS + MODES]
        blocks = [[third[t * p : t * (p + 1), t * q : t * (q + 1)] for q in range(3)] for p in range(3)]
        ends = shared(blocks[1][1], blocks[2][2])
        half = t // 2 + 1
        ends = jnp.concatenate([ends[:, :half], jnp.pad(ends[:, half:], ((0, t), (0, 1)))], axis=0)
        unused = jnp.zeros((COLS, 128 - COLS - 1 - MODES - half), F32)
        pay[0:COLS, :] = jnp.concatenate([shared(first, second), zeroth, ends, unused], axis=1)
        pay[COLS : COLS + t, :] = jnp.concatenate([blocks[0][1], blocks[0][2], blocks[1][2], blocks[0][0]], axis=1)


def own_kernel(nx, ny, nz, info, centers, own, kept_in, base, fext, qext, kept):
    kept[...] = kept_in[...]
    rows = Rows(nx, ny, nz, info, centers, base, fext, qext)
    for layer in range(nx):
        rows.describe([own[k, layer] for k in range(3)], layer + 2, pl.ds(0, ny), 0, True)
    for i in range(2, nx + 2):

        @pl.loop(0, ny, unroll=True)
        def _(j, i=i):
            rows.both(i, j)


def inner_kernel(nx, ny, nz, info, centers, across, pair, base_in, fext_in, qext_in, base, fext, qext, lh, gram, rh):
    del base_in, fext_in, qext_in
    rows = Rows(nx, ny, nz, info, centers, base, fext, qext)
    core = info[4]
    other, beyond = pair[...], across[...]
    before = jnp.where(core == 0, beyond, other)
    after = jnp.where(core == 0, other, beyond)
    for layer in range(nx):
        rows.describe([before[k, layer] for k in range(3)], layer, pl.ds(0, ny), 0, layer == nx - 1)
        rows.describe([after[k, layer] for k in range(3)], layer + 2 + nx, pl.ds(0, ny), 0, layer == 0)
    for i in (0, 1, nx + 2, nx + 3):

        @pl.loop(0, ny, unroll=True)
        def _(j, i=i):
            if i in (1, nx + 2):
                rows.both(i, j)
            else:
                rows.forcing(i, j)

    for i in range(1, nx + 3):

        @pl.loop(1, ny - 1, unroll=True)
        def _(j, i=i):
            rows.operated(i, j)

    for i in range(2, nx + 2):

        @pl.loop(0, ny - 4, unroll=True)
        def _(k, i=i):
            cells = pl.ds(pl.multiple_of(((i - 2) * (ny - 4) + k) * nz, nz), nz)
            rows.collect(i, k + 2, cells, lh, rh)

    gram[...] = dot(lh[...], rh[...], ((1,), (1,)))


def outer_kernel(
    nx, ny, nz, info, centers, odd, even, base_in, fext_in, qext_in, gram, base, fext, qext, lh, pay, rh
):
    del base_in, fext_in, qext_in
    rows = Rows(nx, ny, nz, info, centers, base, fext, qext)
    parity = info[5]
    above = jnp.where(parity == 0, even[...], odd[...])
    below = jnp.where(parity == 0, odd[...], even[...])
    for layer in range(nx + 2):
        rows.describe([above[k, layer] for k in range(3)], layer + 1, pl.ds(ny, 2), ny, True)
        rows.describe([below[k, layer] for k in range(3)], layer + 1, pl.ds(ny + 2, 2), -2, True)
    for i in range(1, nx + 3):
        reach = 2 if 2 <= i < nx + 2 else 1
        for j in list(range(-reach, 0)) + list(range(ny, ny + reach)):
            if j in (-1, ny) and 2 <= i < nx + 2:
                rows.both(i, j)
            else:
                rows.forcing(i, j)
    for i in range(1, nx + 3):
        inside = 2 <= i < nx + 2

        @pl.loop(0, 2, unroll=True)
        def _(k, i=i):
            rows.operated(i, k * (ny - 1))

        if inside:

            @pl.loop(0, 2, unroll=True)
            def _(k, i=i):
                rows.operated(i, k * (ny + 1) - 1)

    for i in range(2, nx + 2):

        @pl.loop(0, 4, unroll=True)
        def _(k, i=i):
            cells = pl.ds(pl.multiple_of(((i - 2) * 4 + k) * nz, nz), nz)
            rows.collect(i, jnp.where(k < 2, k, k + ny - 4), cells, lh, rh)

    rows.pack(gram[...] + dot(lh[...], rh[...], ((1,), (1,))), pay)


def solve_spd(turned, matrix, work):
    size = matrix.shape[0]
    r = lax.broadcasted_iota(jnp.int32, (size, size), 0)
    c = lax.broadcasted_iota(jnp.int32, (size, size), 1)
    diagonal = jnp.where(r == c, matrix, 0.0)
    scale_r = lax.rsqrt(jnp.sum(diagonal, axis=1, keepdims=True))
    scale_c = lax.rsqrt(jnp.sum(diagonal, axis=0, keepdims=True))
    scaled = matrix * scale_r * scale_c
    turned = turned * scale_c
    work[0:size] = scaled
    work[size:] = turned
    product = mm(work[...], scaled)
    square = product[:size]
    bound = jnp.max(jnp.sum(jnp.abs(square), axis=0, keepdims=True), axis=1, keepdims=True)
    weight = lax.rsqrt(bound)
    eye = (r == c).astype(F32)
    work[0:size] = eye - (30.0 / 7.0 * weight) * scaled + (25.0 / 7.0 * weight * weight) * square
    work[size:] = (30.0 / 7.0) * turned - (25.0 / 7.0 * weight) * product[size:]

    def longer(carry):
        power = work[0:size]
        more = mm(work[...], power)
        work[0:size] = more[:size]
        work[size:] = work[size:] + more[size:]
        return carry[0] + 1, jnp.sum(power * power) > 2e-6

    lax.while_loop(lambda carry: (carry[0] < 28) & carry[1], longer, (jnp.int32(0), jnp.bool_(True)))
    return work[size:] * (weight * scale_c)


def solve_kernel(nx, ny, nz, scale, pay, inner, outer, out, added, work):
    zeroth, first, second, third = unpacked(pay)
    center = jnp.where(on_diagonal(COLS), second / first, 0.0)
    shift = jnp.sum(jnp.sum(center, axis=1, keepdims=True), axis=0, keepdims=True) * (1.0 / COLS)
    cross = second - shift * first
    energy = jnp.concatenate(
        [
            jnp.concatenate([first, cross], axis=1),
            jnp.concatenate([cross, third - shift * (second + cross)], axis=1),
        ],
        axis=0,
    )
    solved = solve_spd(jnp.concatenate([zeroth, first - shift * zeroth], axis=1), energy, work)
    later = solved[:, COLS:]
    early = solved[:, :COLS] - shift * later
    coeffs = jnp.concatenate([early, later], axis=1)
    rows = nx * ny
    for lh, places in ((inner, range(2, ny - 2)), (outer, [0, 1, ny - 2, ny - 1])):
        values = mm(coeffs, lh[...])
        for k, (i, j) in enumerate((i, j) for i in range(nx) for j in places):
            out[pl.ds(i * ny + j, COLS, stride=rows), :] = values[:, k * nz : (k + 1) * nz]
    added[...] = (mm(early, zeroth) + mm(later, first)).T * scale


def swap(array, axes, start):
    size = lax.axis_size(axes)
    pairs = [(i, i + 1) for i in range(start, size - 1, 2)]
    return lax.ppermute(array, axes, pairs + [(j, i) for i, j in pairs])


def reduced(part):
    near, far = (lax.axis_size(axes) for axes in (NEAR, FAR))
    rows, lanes = part.shape
    piece = lax.all_to_all(part, NEAR, 0, 0, tiled=True).reshape(near, rows // near, lanes).sum(0)
    piece = lax.all_to_all(jnp.broadcast_to(piece[None], (far,) + piece.shape), FAR, 0, 0, tiled=True).sum(0)
    return lax.all_to_all(
        jnp.broadcast_to(piece[None], (near,) + piece.shape), NEAR, 0, 0, tiled=True
    ).reshape(rows, lanes)


def shards(surface_tags, normal_index, fluid_mask, body_centers):
    nx, ny, nz = surface_tags.shape
    count_x = nx * lax.axis_size(GX)
    count_y = ny * lax.axis_size(GY)
    at_x, at_y, core = lax.axis_index(GX), lax.axis_index(GY), lax.axis_index("c")
    own = lax.optimization_barrier(jnp.stack([surface_tags, normal_index, fluid_mask]))
    across = swap(own, GX, 1)
    pair = lax.ppermute(own, "c", [(0, 1), (1, 0)])
    before = jnp.where(core == 1, pair, across)[:, nx - 1 :]
    after = jnp.where(core == 0, pair, across)[:, :1]
    near = jnp.concatenate([before, own, after], axis=1)
    first, last = near[:, :, :2], near[:, :, ny - 2 :]
    parity = at_y % 2
    even = swap(jnp.where(parity == 0, last, first), GY, 0)
    odd = swap(jnp.where(parity == 0, first, last), GY, 1)
    info = jnp.stack(
        [at_x * nx, at_y * ny, jnp.int32(count_x), jnp.int32(count_y), core, parity]
    ).astype(jnp.int32)
    half = nx * ny * nz // 2
    centers = body_centers.T
    ex, ey = nx + 4, ny + 4
    vmem = pl.BlockSpec(memory_space=pltpu.VMEM)
    smem = pl.BlockSpec(memory_space=pltpu.SMEM)

    def shape(*dims):
        return jax.ShapeDtypeStruct(dims, F32)

    def call(kernel, outs, ins, scratch, flops, aliases, name):
        return pl.pallas_call(
            functools.partial(kernel, nx, ny, nz),
            out_shape=outs,
            in_specs=[smem, smem] + [vmem] * (len(ins) - 2),
            out_specs=tuple(vmem for _ in outs),
            scratch_shapes=scratch,
            input_output_aliases=aliases,
            compiler_params=pltpu.CompilerParams(vmem_limit_bytes=24 * 1024 * 1024),
            cost_estimate=pl.CostEstimate(flops=flops, bytes_accessed=8 * 1024 * 1024, transcendentals=0),
            name=name,
        )(*ins)

    base, field = shape(MASK + 1, ex, ey, nz), shape(ex, ey, COLS, nz)
    base, fext, qext, kept = call(
        own_kernel, (base, field, field, shape(3, BODIES)),
        (info, centers, own, centers), [], 1 << 28, {}, "own_rows",
    )
    rh = [pltpu.VMEM((2 * COLS + MODES, half), F32)]
    base, fext, qext, inner, gram = call(
        inner_kernel,
        (shape(*base.shape), shape(*fext.shape), shape(*qext.shape), shape(2 * COLS, half), shape(2 * COLS, 2 * COLS + MODES)),
        (info, kept, across, pair, base, fext, qext), rh, 1 << 29, {4: 0, 5: 1, 6: 2}, "inner_rows",
    )
    _, _, _, outer, pay = call(
        outer_kernel,
        (shape(*base.shape), shape(*fext.shape), shape(*qext.shape), shape(2 * COLS, half), shape(COLS + THIRD, 128)),
        (info, kept, odd, even, base, fext, qext, gram), rh, 1 << 29, {4: 0, 5: 1, 6: 2}, "outer_rows",
    )
    pay = reduced(pay)
    scale = 8.0 * BODIES / (count_x * count_y * nz)
    pressure, added = pl.pallas_call(
        functools.partial(solve_kernel, nx, ny, nz, scale),
        out_shape=(
            jax.ShapeDtypeStruct((COLS * nx * ny, nz), F32),
            jax.ShapeDtypeStruct((COLS, COLS), F32),
        ),
        in_specs=[vmem] * 3,
        out_specs=(vmem, vmem),
        scratch_shapes=[pltpu.VMEM((3 * COLS, 2 * COLS), F32)],
        compiler_params=pltpu.CompilerParams(vmem_limit_bytes=24 * 1024 * 1024),
        name="solve",
    )(pay, inner, outer)
    return pressure.reshape(COLS, nx, ny, nz), added


def solution(mesh):
    split = Mesh(np.asarray(mesh.devices).reshape(4, 4, 2, 4, 4), GX + GY)
    return jax.shard_map(
        shards,
        mesh=split,
        in_specs=(P(GX, GY, None), P(GX, GY, None), P(GX, GY, None), P()),
        out_specs=(P(None, GX, GY, None), P()),
        check_vma=False,
    )
```

```python
import functools

import jax
import jax.numpy as jnp
import numpy as np
from jax import lax
from jax.experimental import pallas as pl
from jax.experimental.pallas import tpu as pltpu
from jax.sharding import Mesh, PartitionSpec as P

BODIES = 16
MODES = 6
COLS = BODIES * MODES
FOLD = 4 * MODES
GX = ("y", "zh", "c")
GY = ("x", "zl")
NEAR = ("c", "x", "y")
FAR = ("zh", "zl")
F32 = jnp.float32


def dot(left, right, dims):
    return lax.dot_general(
        left, right, (dims, ((), ())), precision=lax.Precision.HIGHEST, preferred_element_type=F32
    )


def mm(left, right):
    return dot(left, right, ((1,), (0,)))


THIRD = COLS // 3
NEXT = MODES + 1
PREVIOUS = 2 * NEXT
MASK = 3 * NEXT


def upper(size):
    r = lax.broadcasted_iota(jnp.int32, (size, size), 0)
    return r <= lax.broadcasted_iota(jnp.int32, (size, size), 1)


def on_diagonal(size):
    r = lax.broadcasted_iota(jnp.int32, (size, size), 0)
    return r == lax.broadcasted_iota(jnp.int32, (size, size), 1)


def same_mode(shape):
    r = lax.broadcasted_iota(jnp.int32, shape, 0)
    c = lax.broadcasted_iota(jnp.int32, shape, 1)
    return (c - MODES * ((c * 43) >> 8) == r).astype(F32)


def shared(left, right):
    size = left.shape[0]
    shape = (size, size + 1)
    r = lax.broadcasted_iota(jnp.int32, shape, 0)
    low = lax.broadcasted_iota(jnp.int32, shape, 1) <= r
    blank = jnp.zeros((size, 1), F32)
    return jnp.where(low, jnp.concatenate([right, blank], axis=1), jnp.concatenate([blank, left], axis=1))


def unshared(both):
    size = both.shape[0]
    left, right = both[:, 1 : size + 1], both[:, 0:size]
    keep = upper(size)
    return jnp.where(keep, left, left.T), jnp.where(keep, right.T, right)


def unpacked(pay):
    t = THIRD
    first, second = unshared(pay[0:COLS, 0 : COLS + 1])
    at = COLS + 1
    r = lax.broadcasted_iota(jnp.int32, (COLS, COLS), 0)
    c = lax.broadcasted_iota(jnp.int32, (COLS, COLS), 1)
    zeroth = mm(pay[0:COLS, at : at + MODES], same_mode((MODES, COLS)))
    zeroth = jnp.where(((r * 43) >> 8) == ((c * 43) >> 8), zeroth, 0.0)
    at, half = at + MODES, t // 2 + 1
    middle, end = unshared(
        jnp.concatenate([pay[0:t, at : at + half], pay[t : 2 * t, at : at + half - 1]], axis=1)
    )
    block = [pay[COLS : COLS + t, t * k : t * (k + 1)] for k in range(4)]
    third = jnp.concatenate(
        [
            jnp.concatenate([block[3], block[0], block[1]], axis=1),
            jnp.concatenate([block[0].T, middle, block[2]], axis=1),
            jnp.concatenate([block[1].T, block[2].T, end], axis=1),
        ],
        axis=0,
    )
    return zeroth, first, second, third


class Rows:
    def __init__(self, nx, ny, nz, info, centers, base, fext, qext):
        self.nx, self.ny, self.nz, self.ey = nx, ny, nz, ny + 4
        self.info, self.centers = info, centers
        self.base, self.fext, self.qext = base, fext, qext
        row = lax.broadcasted_iota(jnp.int32, (FOLD, nz), 0)
        body = (row * 43) >> 8
        mode = row - MODES * body
        self.is_mode = [mode == m for m in range(MODES)]
        self.bodies = [(body + k * (FOLD // MODES)).astype(F32) for k in range(COLS // FOLD)]

    def describe(self, cells, layer, rows, first_y, shifts):
        nz, base, info = self.nz, self.base, self.info
        tags, index, fluid = cells
        lane = lax.broadcasted_iota(jnp.int32, tags.shape, 1)
        y = lax.broadcasted_iota(jnp.int32, tags.shape, 0) + (info[1] + first_y)
        shifted = index + (index >= 13).astype(jnp.int32)
        part_x = (shifted >= 9).astype(jnp.int32) + (shifted >= 18).astype(jnp.int32)
        rest = shifted - 9 * part_x
        part_y = (rest >= 3).astype(jnp.int32) + (rest >= 6).astype(jnp.int32)
        part_z = rest - 3 * part_y
        comps = [(part - 1).astype(F32) for part in (part_x, part_y, part_z)]
        inverse = 1.0 / jnp.sqrt(comps[0] * comps[0] + comps[1] * comps[1] + comps[2] * comps[2])
        fl = fluid.astype(F32)
        active = jnp.where(tags < BODIES, fl, 0.0)
        n_x, n_y, n_z = (comp * inverse * active for comp in comps)
        place = [jnp.zeros(tags.shape, F32)] * 3
        for b in range(BODIES):
            here = tags == b
            place = [jnp.where(here, self.centers[d, b], place[d]) for d in range(3)]
        pos_x = ((info[0] + (layer - 2)).astype(F32) + 0.5) / info[2].astype(F32)
        pos_y = (y.astype(F32) + 0.5) / info[3].astype(F32)
        pos_z = (lane.astype(F32) + 0.5) * (1.0 / nz)
        l_x, l_y, l_z = (3.0 * (pos - center) for pos, center in zip((pos_x, pos_y, pos_z), place))
        values = [n_x, n_y, n_z, l_y * n_z - l_z * n_y, l_z * n_x - l_x * n_z, l_x * n_y - l_y * n_x]
        for m, value in enumerate(values + [tags.astype(F32)]):
            base[m, layer, rows] = value
            if shifts:
                after = pltpu.roll(value, nz - 1, 1)
                before = pltpu.roll(value, 1, 1)
                if m == MODES:
                    after = jnp.where(lane == nz - 1, -1.0, after)
                    before = jnp.where(lane == 0, -1.0, before)
                base[NEXT + m, layer, rows] = after
                base[PREVIOUS + m, layer, rows] = before
        base[MASK, layer, rows] = fl

    def at(self, j):
        return jnp.where(j < 0, j + self.ey, jnp.where(j >= self.ey, j - self.ey, j))

    def row(self, which, i, j, rows):
        return jnp.broadcast_to(self.base[which, i, pl.ds(j, 1), :], (rows, self.nz))

    def sample(self, first, i, j):
        value = self.row(first, i, j, FOLD)
        for m in range(1, MODES):
            value = jnp.where(self.is_mode[m], self.row(first + m, i, j, FOLD), value)
        tag = self.row(first + MODES, i, j, FOLD)
        return jnp.concatenate([jnp.where(tag == bodies, value, 0.0) for bodies in self.bodies], axis=0)

    def forcing(self, i, j):
        j = self.at(j)
        self.fext[i, j] = self.sample(0, i, j)

    def both(self, i, j):
        j = self.at(j)
        self.fext[i, j] = self.sample(0, i, j)
        self.qext[i, j] = self.sample(NEXT, i, j) + self.sample(PREVIOUS, i, j)

    def apply(self, src, i, j, field, along_z):
        beside = src[i + 1, j] + src[i - 1, j]
        beside = beside + src[i, self.at(j + 1)] + src[i, self.at(j - 1)]
        beside = beside + along_z
        return field + self.row(MASK, i, j, COLS) * (5.0 * field - beside)

    def operated(self, i, j):
        j = self.at(j)
        self.qext[i, j] = self.apply(self.fext, i, j, self.fext[i, j], self.qext[i, j])

    def collect(self, i, j, cells, lh, rh):
        nz = self.nz
        lane = lax.broadcasted_iota(jnp.int32, (COLS, nz), 1)
        forcing, field = self.fext[i, j], self.qext[i, j]
        up = jnp.where(lane >= 1, pltpu.roll(field, 1, 1), 0.0)
        down = jnp.where(lane < nz - 1, pltpu.roll(field, nz - 1, 1), 0.0)
        lh[0:COLS, cells] = forcing
        lh[COLS : 2 * COLS, cells] = field
        rh[0:COLS, cells] = field
        rh[COLS : 2 * COLS, cells] = self.apply(self.qext, i, j, field, up + down)
        for m in range(MODES):
            rh[2 * COLS + m : 2 * COLS + m + 1, cells] = self.base[m, i, pl.ds(j, 1), :]


    @staticmethod
    def pack(grams, more, pay):
        first, second = grams[0:COLS, 0:COLS], grams[COLS : 2 * COLS, 0:COLS]
        third = grams[COLS : 2 * COLS, COLS : 2 * COLS] + more
        t = THIRD
        zeroth = grams[0:COLS, 2 * COLS : 2 * COLS + MODES]
        blocks = [[third[t * p : t * (p + 1), t * q : t * (q + 1)] for q in range(3)] for p in range(3)]
        ends = shared(blocks[1][1], blocks[2][2])
        half = t // 2 + 1
        ends = jnp.concatenate([ends[:, :half], jnp.pad(ends[:, half:], ((0, t), (0, 1)))], axis=0)
        unused = jnp.zeros((COLS, 128 - COLS - 1 - MODES - half), F32)
        pay[0:COLS, :] = jnp.concatenate([shared(first, second), zeroth, ends, unused], axis=1)
        pay[COLS : COLS + t, :] = jnp.concatenate([blocks[0][1], blocks[0][2], blocks[1][2], blocks[0][0]], axis=1)


def own_kernel(nx, ny, nz, info, centers, own, kept_in, base, fext, qext, kept):
    kept[...] = kept_in[...]
    rows = Rows(nx, ny, nz, info, centers, base, fext, qext)
    for layer in range(nx):
        rows.describe([own[k, layer] for k in range(3)], layer + 2, pl.ds(0, ny), 0, True)
    for i in range(2, nx + 2):

        @pl.loop(0, ny, unroll=True)
        def _(j, i=i):
            rows.both(i, j)


def inner_kernel(nx, ny, nz, info, centers, across, pair, base_in, fext_in, qext_in, base, fext, qext, lh, gram, rh, lh2, rh2):
    del base_in, fext_in, qext_in
    rows = Rows(nx, ny, nz, info, centers, base, fext, qext)
    core = info[4]
    other, beyond = pair[...], across[...]
    before = jnp.where(core == 0, beyond, other)
    after = jnp.where(core == 0, other, beyond)
    for layer in range(nx):
        rows.describe([before[k, layer] for k in range(3)], layer, pl.ds(0, ny), 0, layer == nx - 1)
        rows.describe([after[k, layer] for k in range(3)], layer + 2 + nx, pl.ds(0, ny), 0, layer == 0)
    for i in (0, 1, nx + 2, nx + 3):

        @pl.loop(0, ny, unroll=True)
        def _(j, i=i):
            if i in (1, nx + 2):
                rows.both(i, j)
            else:
                rows.forcing(i, j)

    for i in range(1, nx + 3):

        @pl.loop(1, ny - 1, unroll=True)
        def _(j, i=i):
            rows.operated(i, j)

    for i in range(2, nx + 2):

        @pl.loop(0, ny - 4, unroll=True)
        def _(k, i=i):
            cells = pl.ds(pl.multiple_of(((i - 2) * (ny - 4) + k) * nz, nz), nz)
            rows.collect(i, k + 2, cells, lh, rh)

    for k, (i, j) in enumerate((i, j) for i in range(nx) for j in (1, ny - 2)):
        cells = slice(k * nz, (k + 1) * nz)
        lh2[0:COLS, cells] = fext[i + 2, j]
        lh2[COLS:, cells] = qext[i + 2, j]
        rh2[0:COLS, cells] = qext[i + 2, j]
        for m in range(MODES):
            rh2[COLS + m : COLS + m + 1, cells] = base[m, i + 2, j : j + 1, :]
    more = dot(lh2[...], rh2[...], ((1,), (1,)))
    gram[...] = dot(lh[...], rh[...], ((1,), (1,)))
    gram[:, 0:COLS] = gram[:, 0:COLS] + more[:, 0:COLS]
    gram[:, 2 * COLS :] = gram[:, 2 * COLS :] + more[:, COLS:]


def outer_kernel(
    nx, ny, nz, info, centers, odd, even, base_in, fext_in, qext_in, gram, base, fext, qext, lh, pay, rh
):
    del base_in, fext_in, qext_in
    rows = Rows(nx, ny, nz, info, centers, base, fext, qext)
    parity = info[5]
    above = jnp.where(parity == 0, even[...], odd[...])
    below = jnp.where(parity == 0, odd[...], even[...])
    for layer in range(nx + 2):
        rows.describe([above[k, layer] for k in range(3)], layer + 1, pl.ds(ny, 2), ny, True)
        rows.describe([below[k, layer] for k in range(3)], layer + 1, pl.ds(ny + 2, 2), -2, True)
    for i in range(1, nx + 3):
        reach = 2 if 2 <= i < nx + 2 else 1
        for j in list(range(-reach, 0)) + list(range(ny, ny + reach)):
            if j in (-1, ny) and 2 <= i < nx + 2:
                rows.both(i, j)
            else:
                rows.forcing(i, j)
    for i in range(1, nx + 3):
        inside = 2 <= i < nx + 2

        @pl.loop(0, 2, unroll=True)
        def _(k, i=i):
            rows.operated(i, k * (ny - 1))

        if inside:

            @pl.loop(0, 2, unroll=True)
            def _(k, i=i):
                rows.operated(i, k * (ny + 1) - 1)

    for k, (i, j) in enumerate((i, j) for pair in ((0, ny - 1), (1, ny - 2)) for i in range(nx) for j in pair):
        rows.collect(i + 2, j, pl.ds(k * nz, nz), lh, rh)
    half = nx * 2 * nz
    grams = gram[...] + dot(lh[:, 0:half], rh[:, 0:half], ((1,), (1,)))
    rows.pack(grams, dot(lh[COLS:, half:], rh[COLS : 2 * COLS, half:], ((1,), (1,))), pay)


def solve_spd(turned, matrix, work):
    size = matrix.shape[0]
    r = lax.broadcasted_iota(jnp.int32, (size, size), 0)
    c = lax.broadcasted_iota(jnp.int32, (size, size), 1)
    diagonal = jnp.where(r == c, matrix, 0.0)
    scale_r = lax.rsqrt(jnp.sum(diagonal, axis=1, keepdims=True))
    scale_c = lax.rsqrt(jnp.sum(diagonal, axis=0, keepdims=True))
    scaled = matrix * scale_r * scale_c
    turned = turned * scale_c
    work[0:size] = scaled
    work[size:] = turned
    product = mm(work[...], scaled)
    square = product[:size]
    bound = jnp.max(jnp.sum(jnp.abs(square), axis=0, keepdims=True), axis=1, keepdims=True)
    weight = lax.rsqrt(bound)
    eye = (r == c).astype(F32)
    work[0:size] = eye - (30.0 / 7.0 * weight) * scaled + (25.0 / 7.0 * weight * weight) * square
    work[size:] = (30.0 / 7.0) * turned - (25.0 / 7.0 * weight) * product[size:]

    def longer(carry):
        power = work[0:size]
        more = mm(work[...], power)
        work[0:size] = more[:size]
        work[size:] = work[size:] + more[size:]
        return carry[0] + 1, jnp.sum(power * power) > 2e-6

    lax.while_loop(lambda carry: (carry[0] < 28) & carry[1], longer, (jnp.int32(0), jnp.bool_(True)))
    return work[size:] * (weight * scale_c)


def solve_kernel(nx, ny, nz, scale, pay, inner, outer, out, added, work):
    zeroth, first, second, third = unpacked(pay)
    center = jnp.where(on_diagonal(COLS), second / first, 0.0)
    shift = jnp.sum(jnp.sum(center, axis=1, keepdims=True), axis=0, keepdims=True) * (1.0 / COLS)
    cross = second - shift * first
    energy = jnp.concatenate(
        [
            jnp.concatenate([first, cross], axis=1),
            jnp.concatenate([cross, third - shift * (second + cross)], axis=1),
        ],
        axis=0,
    )
    solved = solve_spd(jnp.concatenate([zeroth, first - shift * zeroth], axis=1), energy, work)
    later = solved[:, COLS:]
    early = solved[:, :COLS] - shift * later
    coeffs = jnp.concatenate([early, later], axis=1)
    rows = nx * ny
    middle = [(i, j) for i in range(nx) for j in range(2, ny - 2)]
    ends = [(i, j) for pair in ((0, ny - 1), (1, ny - 2)) for i in range(nx) for j in pair]
    for lh, places in ((inner, middle), (outer, ends)):
        values = mm(coeffs, lh[...])
        for k, (i, j) in enumerate(places):
            out[pl.ds(i * ny + j, COLS, stride=rows), :] = values[:, k * nz : (k + 1) * nz]
    added[...] = (mm(early, zeroth) + mm(later, first)).T * scale


def swap(array, axes, start):
    size = lax.axis_size(axes)
    pairs = [(i, i + 1) for i in range(start, size - 1, 2)]
    return lax.ppermute(array, axes, pairs + [(j, i) for i, j in pairs])


def reduced(part):
    near, far = (lax.axis_size(axes) for axes in (NEAR, FAR))
    rows, lanes = part.shape
    piece = lax.all_to_all(part, NEAR, 0, 0, tiled=True).reshape(near, rows // near, lanes).sum(0)
    piece = lax.all_to_all(jnp.broadcast_to(piece[None], (far,) + piece.shape), FAR, 0, 0, tiled=True).sum(0)
    return lax.all_to_all(
        jnp.broadcast_to(piece[None], (near,) + piece.shape), NEAR, 0, 0, tiled=True
    ).reshape(rows, lanes)


def shards(surface_tags, normal_index, fluid_mask, body_centers):
    nx, ny, nz = surface_tags.shape
    count_x = nx * lax.axis_size(GX)
    count_y = ny * lax.axis_size(GY)
    at_x, at_y, core = lax.axis_index(GX), lax.axis_index(GY), lax.axis_index("c")
    own = lax.optimization_barrier(jnp.stack([surface_tags, normal_index, fluid_mask]))
    across = swap(own, GX, 1)
    pair = lax.ppermute(own, "c", [(0, 1), (1, 0)])
    before = jnp.where(core == 1, pair, across)[:, nx - 1 :]
    after = jnp.where(core == 0, pair, across)[:, :1]
    near = jnp.concatenate([before, own, after], axis=1)
    first, last = near[:, :, :2], near[:, :, ny - 2 :]
    parity = at_y % 2
    even = swap(jnp.where(parity == 0, last, first), GY, 0)
    odd = swap(jnp.where(parity == 0, first, last), GY, 1)
    info = jnp.stack(
        [at_x * nx, at_y * ny, jnp.int32(count_x), jnp.int32(count_y), core, parity]
    ).astype(jnp.int32)
    half = nx * ny * nz // 2
    centers = body_centers.T
    ex, ey = nx + 4, ny + 4
    vmem = pl.BlockSpec(memory_space=pltpu.VMEM)
    smem = pl.BlockSpec(memory_space=pltpu.SMEM)

    def shape(*dims):
        return jax.ShapeDtypeStruct(dims, F32)

    def call(kernel, outs, ins, scratch, flops, aliases, name):
        return pl.pallas_call(
            functools.partial(kernel, nx, ny, nz),
            out_shape=outs,
            in_specs=[smem, smem] + [vmem] * (len(ins) - 2),
            out_specs=tuple(vmem for _ in outs),
            scratch_shapes=scratch,
            input_output_aliases=aliases,
            compiler_params=pltpu.CompilerParams(vmem_limit_bytes=24 * 1024 * 1024),
            cost_estimate=pl.CostEstimate(flops=flops, bytes_accessed=8 * 1024 * 1024, transcendentals=0),
            name=name,
        )(*ins)

    base, field = shape(MASK + 1, ex, ey, nz), shape(ex, ey, COLS, nz)
    base, fext, qext, kept = call(
        own_kernel, (base, field, field, shape(3, BODIES)),
        (info, centers, own, centers), [], 1 << 28, {}, "own_rows",
    )
    rh = [pltpu.VMEM((2 * COLS + MODES, half), F32)]
    base, fext, qext, inner, gram = call(
        inner_kernel,
        (shape(*base.shape), shape(*fext.shape), shape(*qext.shape), shape(2 * COLS, half), shape(2 * COLS, 2 * COLS + MODES)),
        (info, kept, across, pair, base, fext, qext), rh + [pltpu.VMEM((2 * COLS, half // 2), F32), pltpu.VMEM((COLS + MODES, half // 2), F32)], 1 << 29, {4: 0, 5: 1, 6: 2}, "inner_rows",
    )
    _, _, _, outer, pay = call(
        outer_kernel,
        (shape(*base.shape), shape(*fext.shape), shape(*qext.shape), shape(2 * COLS, half), shape(COLS + THIRD, 128)),
        (info, kept, odd, even, base, fext, qext, gram), rh, 1 << 29, {4: 0, 5: 1, 6: 2}, "outer_rows",
    )
    pay = reduced(pay)
    scale = 8.0 * BODIES / (count_x * count_y * nz)
    pressure, added = pl.pallas_call(
        functools.partial(solve_kernel, nx, ny, nz, scale),
        out_shape=(
            jax.ShapeDtypeStruct((COLS * nx * ny, nz), F32),
            jax.ShapeDtypeStruct((COLS, COLS), F32),
        ),
        in_specs=[vmem] * 3,
        out_specs=(vmem, vmem),
        scratch_shapes=[pltpu.VMEM((3 * COLS, 2 * COLS), F32)],
        compiler_params=pltpu.CompilerParams(vmem_limit_bytes=24 * 1024 * 1024),
        name="solve",
    )(pay, inner, outer)
    return pressure.reshape(COLS, nx, ny, nz), added


def solution(mesh):
    split = Mesh(np.asarray(mesh.devices).reshape(4, 4, 2, 4, 4), GX + GY)
    return jax.shard_map(
        shards,
        mesh=split,
        in_specs=(P(GX, GY, None), P(GX, GY, None), P(GX, GY, None), P()),
        out_specs=(P(None, GX, GY, None), P()),
        check_vma=False,
    )
```
